256 devices in a mesh: role: 2 (over z_lo), seq: 16 (over z_hi, y), tensor: 8 (over x, core).
Axes of the slice: x: 4, y: 4, z: 8 (z_hi: 4, z_lo: 2; z = z_hi * 2 + z_lo), core: 2. Of those that a mesh axis runs over, the one named last changes fastest.
Arguments:
- queries: bfloat16 [2, 2048, 8192], P('role', 'seq', 'tensor'), may hold values from -6 to 6
- new_kv: bfloat16 [2, 2048, 8, 256], P('role', 'seq', 'tensor'), may hold values from -12 to 12
- prefix_kv: bfloat16 [16384, 8, 256], P('seq', 'tensor'), may hold values from -12 to 12
- cache_kv: bfloat16 [512, 512, 8, 256], P('seq', None, 'tensor'), may hold values from -12 to 12
- prompt_lengths: int32 [8], replicated, may hold values from 1 to 1536, 2048 in all
- cache_lengths: int32 [512], replicated, may hold values from 2 to 512, as said below
- prompt_slots: int32 [8], replicated, may hold values from 0 to 511, as said below
Outputs:
- attended: bfloat16 [2, 2048, 8192], P('role', 'seq', 'tensor')
The draws below stay inside these ranges and needn't reach their ends.
Inputs may be any that keep to these rules, and one draw needn't show every extreme that they name: `prompt_lengths`: the lengths sum to 2048; one is 1536. `cache_lengths`: some row uses all 512 positions. `prompt_slots`: no row takes two prompts; row 0 and row 511 each take one.
All inputs are finite; a program needn't handle non-finite values.
Results may differ from the reference program's by a relative error of at most 0.0045.
Values may be sent and summed in bfloat16 or wider, within the bound.
A program may use at most 192 MiB of HBM per device.

```python
import math
import jax
import jax.numpy as jnp
import numpy as np
from jax import lax

QUERY_HEADS = 64
KEY_VALUE_HEADS = 8
HEAD_WIDTH = 128
QUERY_PER_KEY = 8
PREFIX_LENGTH = 16384
DECODE_TOKENS = 4
DECODE_BATCH = 512
PROMPT_SPAN = 2048
CACHE_CAPACITY = 512
NPROMPT = 8
PMOST = 1536


def bounded_gaussian(key, shape, scale, bound):
    return jnp.clip(scale * jax.random.normal(key, shape, jnp.float32), -bound, bound)


def draw_queries(key, part):
    key = jax.random.fold_in(key, 21)
    value_vectors = bounded_gaussian(key, (2, PROMPT_SPAN, QUERY_HEADS, HEAD_WIDTH), 1.0, 6.0)
    return value_vectors.reshape(2, PROMPT_SPAN, QUERY_HEADS * HEAD_WIDTH).astype(jnp.bfloat16)


def draw_new_kv(key, part):
    key = jax.random.fold_in(key, 22)
    first_random_key, second_random_key = jax.random.split(key)
    key_vectors = bounded_gaussian(first_random_key, (2, PROMPT_SPAN, KEY_VALUE_HEADS, HEAD_WIDTH), 2.5, 12.0)
    value_vectors = bounded_gaussian(second_random_key, (2, PROMPT_SPAN, KEY_VALUE_HEADS, HEAD_WIDTH), 1.0, 6.0)
    return jnp.concatenate([key_vectors, value_vectors], axis=3).astype(jnp.bfloat16)


def draw_prefix_kv(key, part):
    key = jax.random.fold_in(key, 23)
    first_random_key, second_random_key = jax.random.split(key)
    key_vectors = bounded_gaussian(first_random_key, (PREFIX_LENGTH, KEY_VALUE_HEADS, HEAD_WIDTH), 2.5, 12.0)
    value_vectors = bounded_gaussian(second_random_key, (PREFIX_LENGTH, KEY_VALUE_HEADS, HEAD_WIDTH), 1.0, 6.0)
    return jnp.concatenate([key_vectors, value_vectors], axis=2).astype(jnp.bfloat16)


def draw_cache_kv(key, part):
    key = jax.random.fold_in(key, 24)
    first_random_key, second_random_key = jax.random.split(key)
    key_vectors = bounded_gaussian(first_random_key, (DECODE_BATCH, CACHE_CAPACITY, KEY_VALUE_HEADS, HEAD_WIDTH), 2.5, 12.0)
    value_vectors = bounded_gaussian(second_random_key, (DECODE_BATCH, CACHE_CAPACITY, KEY_VALUE_HEADS, HEAD_WIDTH), 1.0, 6.0)
    return jnp.concatenate([key_vectors, value_vectors], axis=3).astype(jnp.bfloat16)


def draw_cache_lengths(key, part):
    key = jax.random.fold_in(key, 31)
    first_random_key, second_random_key, third_key, fourth_key = jax.random.split(key, 4)
    first_piece = jax.random.randint(first_random_key, (DECODE_BATCH,), 2, CACHE_CAPACITY + 1)
    second = jax.random.randint(second_random_key, (DECODE_BATCH,), 2, CACHE_CAPACITY + 1)
    picks = jax.random.randint(third_key, (DECODE_BATCH,), 0, 2)
    lengths = jnp.where(picks == 0, first_piece, jnp.minimum(first_piece, second))
    longest = jax.random.randint(fourth_key, (), 0, DECODE_BATCH)
    return lengths.at[longest].set(CACHE_CAPACITY).astype(jnp.int32)


def draw_prompt_slots(key, part):
    key = jax.random.fold_in(key, 32)
    first_random_key, second_random_key = jax.random.split(key)
    middle_rows = jax.random.permutation(first_random_key, DECODE_BATCH - 2)[:NPROMPT - 2].astype(jnp.int32) + 1
    end_rows = jnp.array([0, DECODE_BATCH - 1], dtype=jnp.int32)
    slots = jnp.concatenate([end_rows, middle_rows])
    return jax.random.permutation(second_random_key, slots).astype(jnp.int32)


def length_profile(amount, total, limit, lean):
    weights = [(1 << 20) // math.isqrt(standing ** lean) + 1 for standing in range(2, amount + 1)]
    rest, holding = total - limit - (amount - 1), [1] * (amount - 1)
    while rest > 0:
        candidates = [i for i in range(amount - 1) if holding[i] < limit]
        mass, remaining = sum([weights[i] for i in candidates]), rest
        for i in candidates:
            extra = min(limit - holding[i], max(1, remaining * weights[i] // mass), rest)
            holding[i] = holding[i] + extra
            rest = rest - extra
    return np.array([limit] + holding)


def uneven(stream_key, amount, total, limit, lean):
    if amount == 2:
        one = jax.random.randint(stream_key, (), max(1, total - limit), min(limit, total - 1) + 1)
        return jnp.stack([one, total - one])
    sizes = jnp.asarray(length_profile(amount, total, limit, lean), jnp.int32)
    pairs = (amount - 1) // 2
    giver, receiver = sizes[1:1 + 2 * pairs:2], sizes[2:2 + 2 * pairs:2]
    slack = jnp.minimum(giver - 1, limit - receiver)
    moved = jax.random.randint(jax.random.fold_in(stream_key, 1), (pairs,), 0, 1 << 20) % (slack + 1)
    sizes = sizes.at[1:1 + 2 * pairs:2].set(giver - moved).at[2:2 + 2 * pairs:2].set(receiver + moved)
    return sizes[jax.random.permutation(jax.random.fold_in(stream_key, 2), amount)]


def setup_inputs(seed: int = 0) -> dict:
    arg_keys = jax.random.split(jax.random.key(seed), 8)
    return {
        "queries": draw_queries(jax.random.fold_in(arg_keys[7], 71), 0),
        "new_kv": draw_new_kv(jax.random.fold_in(arg_keys[7], 71), 0),
        "prefix_kv": draw_prefix_kv(jax.random.fold_in(arg_keys[7], 71), 0),
        "cache_kv": draw_cache_kv(jax.random.fold_in(arg_keys[7], 71), 0),
        "prompt_lengths": uneven(arg_keys[4], NPROMPT, PROMPT_SPAN, PMOST, 2).astype(jnp.int32),
        "cache_lengths": draw_cache_lengths(jax.random.fold_in(arg_keys[7], 71), 0),
        "prompt_slots": draw_prompt_slots(jax.random.fold_in(arg_keys[7], 71), 0),
    }


LOWEST = -1e30


def segment_of(prompt_lengths, count):
    ends = jnp.cumsum(prompt_lengths).astype(jnp.int32)
    places = jnp.arange(count, dtype=jnp.int32)
    return jnp.sum((places[:, None] >= ends[None, :]).astype(jnp.int32), axis=1).astype(jnp.int32)


def prompt_of_row(prompt_slots, count):
    row_ids = jnp.arange(count, dtype=jnp.int32)
    labels = jnp.arange(1, prompt_slots.shape[0] + 1, dtype=jnp.int32)
    hits = jnp.where(prompt_slots[None, :] == row_ids[:, None], labels[None, :], 0)
    return (jnp.sum(hits, axis=1) - 1).astype(jnp.int32)


def attend_heads(query_vector, index_pairs, visible_mask):
    key_vectors = jnp.transpose(index_pairs[:, :, :HEAD_WIDTH], (1, 0, 2)).astype(jnp.float32)
    value_vectors = jnp.transpose(index_pairs[:, :, HEAD_WIDTH:], (1, 0, 2)).astype(jnp.float32)
    scores = jnp.einsum('hrd,hnd->hrn', query_vector.astype(jnp.float32), key_vectors) * (HEAD_WIDTH ** -0.5)
    scores = jnp.where(visible_mask[None], scores, LOWEST)
    highest = jnp.max(scores, axis=2, keepdims=True)
    weights = jnp.where(visible_mask[None], jnp.exp(scores - highest), 0.0)
    total = jnp.sum(weights, axis=2, keepdims=True)
    rounded = weights.astype(jnp.bfloat16).astype(jnp.float32)
    mixed = jnp.einsum('hrn,hnd->hrd', rounded, value_vectors)
    return mixed / total


def prefill(prompt_span_queries, stretch_kv, prefix_kv, segment):
    spread_width = min(PROMPT_SPAN, 32)
    blocks = PROMPT_SPAN // spread_width
    every_position = jnp.concatenate([prefix_kv, stretch_kv], axis=0)
    places = jnp.arange(PROMPT_SPAN, dtype=jnp.int32)

    def one_block(index):
        first_piece = index * spread_width
        row_ids = first_piece + jnp.arange(spread_width, dtype=jnp.int32)
        mine = lax.dynamic_slice_in_dim(segment, first_piece, spread_width)
        query_vector = lax.dynamic_slice_in_dim(prompt_span_queries, first_piece, spread_width).reshape(spread_width, KEY_VALUE_HEADS, QUERY_PER_KEY, HEAD_WIDTH)
        query_vector = jnp.transpose(query_vector, (1, 0, 2, 3)).reshape(KEY_VALUE_HEADS, spread_width * QUERY_PER_KEY, HEAD_WIDTH)
        inner = (places[None, :] <= row_ids[:, None]) & (segment[None, :] == mine[:, None])
        visible_mask = jnp.concatenate([jnp.ones((spread_width, PREFIX_LENGTH), jnp.bool_), inner], axis=1)
        visible_mask = jnp.repeat(visible_mask, QUERY_PER_KEY, axis=0)
        attention_output = attend_heads(query_vector, every_position, visible_mask).reshape(KEY_VALUE_HEADS, spread_width, QUERY_PER_KEY, HEAD_WIDTH)
        return jnp.transpose(attention_output, (1, 0, 2, 3)).reshape(spread_width, QUERY_HEADS * HEAD_WIDTH)

    return lax.map(one_block, jnp.arange(blocks, dtype=jnp.int32)).reshape(PROMPT_SPAN, QUERY_HEADS * HEAD_WIDTH)


def decode(decode_query_rows, fresh_kv, stretch_kv, cache_kv, cache_lengths, prompt_row, segment):
    places = jnp.arange(CACHE_CAPACITY, dtype=jnp.int32)
    step_ids = jnp.arange(DECODE_TOKENS, dtype=jnp.int32)
    step_visible = step_ids[None, :] <= step_ids[:, None]

    def one_row(row_number):
        query_vector = lax.dynamic_slice_in_dim(decode_query_rows, row_number * DECODE_TOKENS, DECODE_TOKENS).reshape(DECODE_TOKENS, KEY_VALUE_HEADS, QUERY_PER_KEY, HEAD_WIDTH)
        query_vector = jnp.transpose(query_vector, (1, 0, 2, 3)).reshape(KEY_VALUE_HEADS, DECODE_TOKENS * QUERY_PER_KEY, HEAD_WIDTH)
        cache = lax.dynamic_index_in_dim(cache_kv, row_number, 0, keepdims=False)
        fresh = lax.dynamic_slice_in_dim(fresh_kv, row_number * DECODE_TOKENS, DECODE_TOKENS)
        index_pairs = jnp.concatenate([cache, stretch_kv, fresh], axis=0)
        length = lax.dynamic_index_in_dim(cache_lengths, row_number, 0, keepdims=False)
        prompt = lax.dynamic_index_in_dim(prompt_row, row_number, 0, keepdims=False)
        visible_mask = jnp.concatenate([
            jnp.broadcast_to((places < length)[None, :], (DECODE_TOKENS, CACHE_CAPACITY)),
            jnp.broadcast_to((segment == prompt)[None, :], (DECODE_TOKENS, PROMPT_SPAN)),
            step_visible], axis=1)
        visible_mask = jnp.repeat(visible_mask, QUERY_PER_KEY, axis=0)
        attention_output = attend_heads(query_vector, index_pairs, visible_mask).reshape(KEY_VALUE_HEADS, DECODE_TOKENS, QUERY_PER_KEY, HEAD_WIDTH)
        return jnp.transpose(attention_output, (1, 0, 2, 3)).reshape(DECODE_TOKENS, QUERY_HEADS * HEAD_WIDTH)

    return lax.map(one_row, jnp.arange(DECODE_BATCH, dtype=jnp.int32)).reshape(PROMPT_SPAN, QUERY_HEADS * HEAD_WIDTH)


def reference(queries, new_kv, prefix_kv, cache_kv, prompt_lengths, cache_lengths, prompt_slots):
    segment = segment_of(prompt_lengths, PROMPT_SPAN)
    prompt_row = prompt_of_row(prompt_slots, DECODE_BATCH)
    prefill_rows = prefill(queries[0], new_kv[0], prefix_kv, segment)
    decode_rows = decode(queries[1], new_kv[1], new_kv[0], cache_kv, cache_lengths, prompt_row, segment)
    return jnp.stack([prefill_rows, decode_rows]).astype(jnp.bfloat16)
```

```python
import functools
import math

import jax
import jax.numpy as jnp
from jax import lax
from jax.experimental import pallas as pl
from jax.experimental.pallas import tpu as pltpu
from jax.sharding import PartitionSpec as P

MESH = pl.DeviceIdType.MESH
NEG = -1e30
D = 128
SCALE = math.log2(math.e) / math.sqrt(D)
RB = 256
NT = (((1,), (1,)), ((), ()))
NN = (((1,), (0,)), ((), ()))
F32 = jnp.float32
BF16 = jnp.bfloat16


def dot(a, b, dims):
    return lax.dot_general(a, b, dims, preferred_element_type=F32)


def with_ones(v):
    return jnp.concatenate([v, jnp.ones_like(v)], axis=1)


def column(row):
    return jnp.transpose(jnp.broadcast_to(row, (D, D)))


def kernel(
    lengths_ref, cache_len_ref, slots_ref, q_ref, new_ref, prefix_ref, cache_ref,
    out_ref,
    kvb, qall, strall, acc, m, l, ob, ls, ro, rl, cacheb, sa, sb, ma, mb,
    pq, pacc, pm, psum,
    local_sem, cache_sem, kv_send, kv_recv, q_send, q_recv, str_send, str_recv,
    slab_send, slab_recv, o_send, o_recv, l_send, l_recv,
):
    role = lax.axis_index("role")
    seq = lax.axis_index("seq")
    tensor = lax.axis_index("tensor")
    zh, y = seq // 4, lax.rem(seq, 4)
    z = zh * 2 + role

    def dev(dy, dz):
        yy = lax.rem(y + dy + 8, 4)
        zz = lax.rem(z + dz + 8, 8)
        return (lax.rem(zz, 2), (zz // 2) * 4 + yy, tensor)

    def remote(src, dst, ss, rs, dy, dz):
        return pltpu.make_async_remote_copy(
            src_ref=src, dst_ref=dst, send_sem=ss, recv_sem=rs,
            device_id=dev(dy, dz), device_id_type=MESH,
        )

    is_pre = role == 0
    is_dec = role == 1
    half = 512

    own_kv = pltpu.make_async_copy(prefix_ref, kvb.at[0], local_sem.at[0])
    own_kv.start()
    own_q = pltpu.make_async_copy(q_ref, qall.at[pl.ds(0, 1024)], local_sem.at[1])
    own_q.start()

    def cache_copy(g):
        rows = pl.ds(g * 4, 4)
        return pltpu.make_async_copy(cache_ref.at[rows], cacheb.at[rows], cache_sem.at[g])

    @pl.when(is_dec)
    def _():
        for g in range(8):
            cache_copy(g).start()

    barrier = pltpu.get_barrier_semaphore()
    peers = [(0, dz) for dz in range(1, 8)] + [(1, 0), (2, 0), (3, 0)]
    for dy, dz in peers:
        pl.semaphore_signal(barrier, inc=1, device_id=dev(dy, dz), device_id_type=MESH)
    pl.semaphore_wait(barrier, len(peers))

    slot = strall.at[zh, y]
    stretch_y = [remote(slot, slot, str_send.at[i], str_recv.at[i], dy, 0) for i, dy in enumerate((1, 3, 2))]
    stretch_z = remote(slot, slot, str_send.at[3], str_recv.at[3], 0, 1)
    first, second = pl.ds(0, half), pl.ds(half, half)
    kv_copies = [
        remote(kvb.at[0, first], kvb.at[1, first], kv_send.at[0], kv_recv.at[0], 1, 0),
        remote(kvb.at[0, second], kvb.at[1, second], kv_send.at[1], kv_recv.at[1], 3, 0),
        remote(kvb.at[0, second], kvb.at[2, first], kv_send.at[2], kv_recv.at[2], 1, 0),
        remote(kvb.at[0, first], kvb.at[2, second], kv_send.at[3], kv_recv.at[3], 3, 0),
        remote(kvb.at[1, first], kvb.at[3, first], kv_send.at[4], kv_recv.at[4], 1, 0),
        remote(kvb.at[1, second], kvb.at[3, second], kv_send.at[5], kv_recv.at[5], 3, 0),
    ]
    far_q = qall.at[pl.ds(1024, 1024)]
    far_half = qall.at[pl.ds(2048, half)]
    q_copies = [
        remote(qall.at[pl.ds(0, 1024)], far_q, q_send.at[0], q_recv.at[0], 0, -1),
        remote(qall.at[pl.ds(0, 1024)], far_q, q_send.at[1], q_recv.at[0], 0, 2),
        remote(qall.at[pl.ds(0, half)], far_half, q_send.at[2], q_recv.at[1], 0, -3),
        remote(qall.at[pl.ds(half, half)], far_half, q_send.at[3], q_recv.at[1], 0, 4),
    ]
    slab = strall.at[zh]
    slab_copies = [
        remote(slab, slab, slab_send.at[i], slab_recv.at[i], 0, dz) for i, dz in enumerate((2, -2, 4))
    ]

    @pl.when(is_pre)
    def _():
        strall[zh, y] = new_ref[...]
        stretch_z.start()
        for c in stretch_y:
            c.start()

    own_kv.wait()
    for c in kv_copies[:4]:
        c.start()
    own_q.wait()

    @pl.when(is_pre)
    def _():
        for c in q_copies:
            c.start()

    def clear(b, _):
        rows = pl.ds(pl.multiple_of(b * D, D), D)
        acc[rows, :] = jnp.zeros((D, D), F32)
        l[rows, :] = jnp.zeros((D, D), F32)
        m[rows, :] = jnp.full((D, D), NEG, F32)
        return 0

    lax.fori_loop(0, 20, clear, 0)

    def block(row0, i):
        return pl.ds(pl.multiple_of(row0 + i * RB, RB), RB)

    def scores(rows, kvi, s, mx):
        x = dot(qall[rows, :], kvb[kvi, :, :D], NT)
        s[...] = x
        mx[...] = jnp.broadcast_to(jnp.max(x, axis=1, keepdims=True) * SCALE, mx.shape)

    def absorb(rows, kvi, s, mx):
        old = m[rows, :]
        new = jnp.maximum(old, mx[...])
        shrink = jnp.exp2(old - new)
        m[rows, :] = new
        p = jnp.exp2(s[...] * SCALE - new[:, :1]).astype(BF16)
        r = dot(p, with_ones(kvb[kvi, :, D:]), NN)
        l[rows, :] = l[rows, :] * shrink + r[:, D:]
        acc[rows, :] = acc[rows, :] * shrink + r[:, :D]

    def attend(row0, n, kvi):
        @pl.when(n > 0)
        def _():
            scores(block(row0, 0), kvi, sa, ma)

            def pair(j, _):
                scores(block(row0, 2 * j + 1), kvi, sb, mb)
                absorb(block(row0, 2 * j), kvi, sa, ma)
                scores(block(row0, jnp.minimum(2 * j + 2, n - 1)), kvi, sa, ma)
                absorb(block(row0, 2 * j + 1), kvi, sb, mb)
                return 0

            lax.fori_loop(0, n // 2, pair, 0)

    ends = []
    running = jnp.int32(0)
    for p in range(8):
        running = running + lengths_ref[p]
        ends.append(running)
    starts = [jnp.int32(0)] + ends[:-1]

    def small(qv, kv_value, mask, rows, m_ref, l_ref, acc_ref):
        s = jnp.where(mask, dot(qv, kv_value[:, :D], NT) * SCALE, NEG)
        old = m_ref[rows, :]
        new = jnp.maximum(old, jnp.max(s, axis=1, keepdims=True))
        shrink = jnp.exp2(old - new)
        p = jnp.where(mask, jnp.exp2(s - new[:, :1]), 0.0).astype(BF16)
        r = dot(p, with_ones(kv_value[:, D:]), NN)
        m_ref[rows, :] = new
        l_ref[rows, :] = l_ref[rows, :] * shrink + r[:, D:]
        acc_ref[rows, :] = acc_ref[rows, :] * shrink + r[:, :D]

    def stretch_block(i, _):
        rows = block(0, i)
        index = lax.broadcasted_iota(jnp.int32, (RB, 1), 0) + i * RB
        own = i < 4
        near = i < 8
        home_zh = jnp.where(own, zh, jnp.where(near, zh + jnp.where(is_pre, 3, 1), zh + 2))
        home_zh = lax.rem(home_zh, 4)
        local = jnp.where(own, 0, jnp.where(near, 1024, jnp.where(is_pre, 2048 - half, 2048)))
        index = index - local
        place = (home_zh * 4 + y) * 128 + (index // 32) * 4 + lax.rem(index, 4)
        begin = jnp.zeros_like(place)
        for e in ends[:-1]:
            begin = jnp.where(place >= e, e, begin)
        keys = lax.broadcasted_iota(jnp.int32, (RB, half), 1) + zh * half
        mask = (keys >= begin) & (keys <= place)
        kv_value = strall[zh].reshape(half, 2 * D)
        small(qall[rows, :], kv_value, mask, rows, m, l, acc)
        return 0

    first_row = seq * 32

    def fresh_block(i, _):
        rows = block(0, i)
        index = lax.broadcasted_iota(jnp.int32, (RB, D), 0) + i * RB
        key = lax.broadcasted_iota(jnp.int32, (RB, D), 1)
        mask = (key // 4 == index // 32) & (lax.rem(key, 4) <= lax.rem(index, 4))
        small(qall[rows, :], new_ref[...], mask, rows, m, l, acc)
        return 0

    def cache_rows(g, _):
        for u in range(4):
            r = g * 4 + u
            rows = pl.ds(pl.multiple_of(r * 32, 32), 32)
            length = cache_len_ref[first_row + r]
            mask = lax.broadcasted_iota(jnp.int32, (32, half), 1) < length
            small(qall[rows, :], cacheb[r], mask, rows, m, l, acc)
        return 0

    def decode_first():
        lax.fori_loop(0, 1024 // RB, fresh_block, 0)
        for g in range(4):
            cache_copy(g).wait()
        lax.fori_loop(0, 4, cache_rows, 0)
        stretch_z.wait_recv()
        for c in stretch_y:
            c.start()
        for g in range(4, 8):
            cache_copy(g).wait()
        lax.fori_loop(4, 8, cache_rows, 0)

    def decode_last():
        for c in slab_copies:
            c.wait_recv()
        owner = lax.broadcasted_iota(jnp.int32, (256, 1), 0) // 32
        target = lax.rem(lax.broadcasted_iota(jnp.int32, (256, 1), 0), 32)
        for p in range(8):
            target = jnp.where(owner == p, target + (slots_ref[p] - first_row) * 32, target)
        chosen = lax.broadcasted_iota(jnp.int32, (256, 1024), 1) == target
        chosen = jnp.where(chosen, 1.0, 0.0).astype(BF16)
        pq[...] = dot(chosen, qall[pl.ds(0, 1024), :], NN).astype(BF16)
        pacc[...] = jnp.zeros_like(pacc)
        psum[...] = jnp.zeros_like(psum)
        pm[...] = jnp.full_like(pm, NEG)
        low = jnp.zeros_like(owner)
        high = jnp.zeros_like(owner)
        for p in range(8):
            low = jnp.where(owner == p, starts[p], low)
            high = jnp.where(owner == p, ends[p], high)

        def one(c, _):
            keys = lax.broadcasted_iota(jnp.int32, (256, half), 1) + c * half
            mask = (keys >= low) & (keys < high)
            small(pq[...], strall[c].reshape(half, 2 * D), mask, pl.ds(0, 256), pm, psum, pacc)
            return 0

        lax.fori_loop(0, 4, one, 0)

        total = psum[...]
        pm[...] = pm[...] + jnp.log2(total)
        pacc[...] = pacc[...] / total

        def merge(r, _):
            rows = pl.ds(pl.multiple_of(r * 32, 32), 32)
            other = jnp.full((32, D), NEG, F32)
            value = jnp.zeros((32, D), F32)
            for p in range(8):
                theirs = pl.ds(p * 32, 32)
                hit = jnp.full((32, D), slots_ref[p] - first_row - r, jnp.int32) == 0
                other = jnp.where(hit, pm[theirs, :], other)
                value = jnp.where(hit, pacc[theirs, :], value)
            old = m[rows, :]
            new = jnp.maximum(old, other)
            w0 = jnp.exp2(old - new)
            w1 = jnp.exp2(other - new)
            mixed = acc[rows, :] * w0 + value * w1
            out_ref[rows, :] = (mixed / (l[rows, :] * w0 + w1)).astype(BF16)
            return 0

        lax.fori_loop(0, 32, merge, 0)

    near_o, far_o = ob.at[pl.ds(0, 1024)], ob.at[pl.ds(1024, half)]
    o_copies_pre = [
        remote(far_o, ro.at[2, second], o_send.at[1], o_recv.at[3], 0, -4),
        remote(ls.at[1], rl.at[3], l_send.at[1], l_recv.at[3], 0, -4),
        remote(near_o, ro.at[1], o_send.at[0], o_recv.at[1], 0, -2),
        remote(ls.at[0], rl.at[1], l_send.at[0], l_recv.at[1], 0, -2),
    ]
    o_copies_dec = [
        remote(far_o, ro.at[2, first], o_send.at[1], o_recv.at[2], 0, 3),
        remote(ls.at[1], rl.at[2], l_send.at[1], l_recv.at[2], 0, 3),
        remote(near_o, ro.at[0], o_send.at[0], o_recv.at[0], 0, 1),
        remote(ls.at[0], rl.at[0], l_send.at[0], l_recv.at[0], 0, 1),
    ]

    def finish_block(b, _):
        rows = pl.ds(pl.multiple_of(1024 + b * D, D), D)
        total = l[rows, :]
        ob[pl.ds(pl.multiple_of(b * D, D), D), :] = (acc[rows, :] / total).astype(BF16)
        stat = jnp.transpose(m[rows, :] + jnp.log2(total))
        ls[b // 8, pl.ds(lax.rem(b, 8), 1), :] = stat[:1, :]
        return 0

    def send_results():
        ls[1, pl.ds(4, 4), :] = jnp.zeros((4, D), F32)
        lax.fori_loop(8, 12, finish_block, 0)

        @pl.when(is_pre)
        def _():
            for c in o_copies_pre[:2]:
                c.start()

        @pl.when(is_dec)
        def _():
            for c in o_copies_dec[:2]:
                c.start()

        lax.fori_loop(0, 8, finish_block, 0)

        @pl.when(is_pre)
        def _():
            for c in o_copies_pre[2:]:
                c.start()

        @pl.when(is_dec)
        def _():
            for c in o_copies_dec[2:]:
                c.start()

    def combine():
        for c in (o_copies_dec[2], o_copies_dec[3], o_copies_pre[2], o_copies_pre[3],
                  o_copies_dec[0], o_copies_dec[1], o_copies_pre[0], o_copies_pre[1]):
            c.wait_recv()

        def one(b, _):
            rows = pl.ds(pl.multiple_of(b * D, D), D)
            total = l[rows, :]
            stats = [m[rows, :] + jnp.log2(total)]
            values = [acc[rows, :] / total]
            for i in range(3):
                if i < 2:
                    row = rl[i, pl.ds(b, 1), :]
                else:
                    row = rl[2 + b // 4, pl.ds(lax.rem(b, 4), 1), :]
                stats.append(column(row))
                values.append(ro[i, rows, :].astype(F32))
            top = functools.reduce(jnp.maximum, stats)
            weights = [jnp.exp2(x - top) for x in stats]
            mixed = functools.reduce(jnp.add, [w * v for w, v in zip(weights, values)])
            out_ref[rows, :] = (mixed / functools.reduce(jnp.add, weights)).astype(BF16)
            return 0

        lax.fori_loop(0, 8, one, 0)

    def step(i, _):
        @pl.when(i == 1)
        def _():
            for c in kv_copies[:2]:
                c.wait_recv()
            for c in kv_copies[4:]:
                c.start()

        @pl.when(i == 2)
        def _():
            q_copies[0].wait_recv()
            q_copies[2].wait_recv()

        @pl.when(i == 4)
        def _():
            for c in kv_copies[2:4]:
                c.wait_recv()

        @pl.when(i == 5)
        def _():
            for c in kv_copies[4:]:
                c.wait_recv()

        @pl.when((i == 0) & is_dec)
        def _():
            decode_first()

        kvi = jnp.where(i < 2, i, jnp.where(i < 4, i - 2, jnp.where(i == 4, 2, 3)))
        only_own = (i < 2) | (i == 6)
        everything = (i == 4) & is_pre
        row0 = jnp.where(only_own | everything, 0, 1024)
        n_own = jnp.where(is_pre, 1024 // RB, 0)
        n = jnp.where(only_own, n_own, jnp.where(everything, 2560 // RB, 1536 // RB))
        attend(row0, n, kvi)

        @pl.when(i == 2)
        def _():
            for c in stretch_y:
                c.wait_recv()

            @pl.when(is_dec)
            def _():
                for c in slab_copies:
                    c.start()

        @pl.when(i == 3)
        def _():
            lax.fori_loop(jnp.where(is_pre, 0, 1024 // RB), 2560 // RB, stretch_block, 0)

        @pl.when(i == 5)
        def _():
            send_results()

        return 0

    lax.fori_loop(0, 7, step, 0)

    @pl.when(is_pre)
    def _():
        combine()

    @pl.when(is_dec)
    def _():
        decode_last()

    for c in kv_copies + stretch_y:
        c.wait_send()

    @pl.when(is_pre)
    def _():
        for c in [stretch_z] + q_copies + o_copies_pre:
            c.wait_send()

    @pl.when(is_dec)
    def _():
        for c in slab_copies + o_copies_dec:
            c.wait_send()


def body(queries, new_kv, prefix_kv, cache_kv, prompt_lengths, cache_lengths, prompt_slots):
    q = queries.reshape(32, 4, 8, D).transpose(0, 2, 1, 3).reshape(1024, D)
    new = new_kv.reshape(128, 2 * D)
    prefix = prefix_kv.reshape(1024, 2 * D)
    cache = cache_kv.reshape(32, 512, 2 * D)
    smem = pl.BlockSpec(memory_space=pltpu.SMEM)
    vmem = pl.BlockSpec(memory_space=pltpu.VMEM)
    hbm = pl.BlockSpec(memory_space=pl.ANY)
    dma = pltpu.SemaphoreType.DMA
    out = pl.pallas_call(
        kernel,
        out_shape=jax.ShapeDtypeStruct((1024, D), BF16),
        in_specs=[smem, smem, smem, hbm, vmem, hbm, hbm],
        out_specs=vmem,
        scratch_shapes=[
            pltpu.VMEM((4, 1024, 2 * D), BF16),
            pltpu.VMEM((2560, D), BF16),
            pltpu.VMEM((4, 4, 128, 2 * D), BF16),
            pltpu.VMEM((2560, D), F32),
            pltpu.VMEM((2560, D), F32),
            pltpu.VMEM((2560, D), F32),
            pltpu.VMEM((1536, D), BF16),
            pltpu.VMEM((2, 8, D), F32),
            pltpu.VMEM((3, 1024, D), BF16),
            pltpu.VMEM((4, 8, D), F32),
            pltpu.VMEM((32, 512, 2 * D), BF16),
            pltpu.VMEM((RB, 1024), F32),
            pltpu.VMEM((RB, 1024), F32),
            pltpu.VMEM((RB, D), F32),
            pltpu.VMEM((RB, D), F32),
            pltpu.VMEM((256, D), BF16),
            pltpu.VMEM((256, D), F32),
            pltpu.VMEM((256, D), F32),
            pltpu.VMEM((256, D), F32),
            dma((2,)), dma((8,)), dma((6,)), dma((6,)), dma((4,)), dma((2,)),
            dma((4,)), dma((4,)), dma((3,)), dma((3,)), dma((2,)), dma((4,)),
            dma((2,)), dma((4,)),
        ],
        compiler_params=pltpu.CompilerParams(
            collective_id=0, has_side_effects=True, vmem_limit_bytes=48 * 2**20
        ),
        cost_estimate=pl.CostEstimate(flops=10**10, bytes_accessed=10**7, transcendentals=10**7),
    )(prompt_lengths, cache_lengths, prompt_slots, q, new, prefix, cache)
    return out.reshape(32, 8, 4, D).transpose(0, 2, 1, 3).reshape(1, 128, 1024)


def solution(mesh):
    return jax.shard_map(
        body,
        mesh=mesh,
        in_specs=(
            P("role", "seq", "tensor"),
            P("role", "seq", "tensor", None),
            P("seq", "tensor", None),
            P("seq", None, "tensor", None),
            P(),
            P(),
            P(),
        ),
        out_specs=P("role", "seq", "tensor"),
        check_vma=False,
    )
```

```python
import functools
import math

import jax
import jax.numpy as jnp
from jax import lax
from jax.experimental import pallas as pl
from jax.experimental.pallas import tpu as pltpu
from jax.sharding import PartitionSpec as P

MESH = pl.DeviceIdType.MESH
NEG = -1e30
D = 128
SCALE = math.log2(math.e) / math.sqrt(D)
RB = 256
NT = (((1,), (1,)), ((), ()))
NN = (((1,), (0,)), ((), ()))
F32 = jnp.float32
BF16 = jnp.bfloat16


def dot(a, b, dims):
    return lax.dot_general(a, b, dims, preferred_element_type=F32)


def with_ones(v):
    return jnp.concatenate([v, jnp.ones_like(v)], axis=1)


def column(row):
    return jnp.transpose(jnp.broadcast_to(row, (D, D)))


def kernel(
    lengths_hbm, cache_len_hbm, slots_hbm, q_ref, new_hbm, prefix_ref, cache_ref,
    out_ref,
    kvb, qall, acc, m, l, ob, ls, ro, rl, rof, rlf, cacheb, sa, sb, ma, mb,
    pqall, pacc, pm, psum, pob, pls, pback, plback, new_ref, lengths_ref, cache_len_ref, slots_ref,
    local_sem, cache_sem, kv_send, kv_recv, q_send, q_recv, str_send, str_recv,
    p_send, p_recv, pb_send, pb_recv, o_send, o_recv, l_send, l_recv,
):
    role = lax.axis_index("role")
    seq = lax.axis_index("seq")
    tensor = lax.axis_index("tensor")
    zh, y = seq // 4, lax.rem(seq, 4)
    z = zh * 2 + role

    def dev(dy, dz):
        yy = lax.rem(y + dy + 8, 4)
        zz = lax.rem(z + dz + 8, 8)
        return (lax.rem(zz, 2), (zz // 2) * 4 + yy, tensor)

    def remote(src, dst, ss, rs, dy, dz):
        return pltpu.make_async_remote_copy(
            src_ref=src, dst_ref=dst, send_sem=ss, recv_sem=rs,
            device_id=dev(dy, dz), device_id_type=MESH,
        )

    is_pre = role == 0
    is_dec = role == 1
    half = 512

    own_kv = pltpu.make_async_copy(prefix_ref, kvb.at[pl.ds(0, 1024)], local_sem.at[0])
    own_kv.start()
    own_q = pltpu.make_async_copy(q_ref, qall.at[pl.ds(0, 1024)], local_sem.at[1])
    own_q.start()
    own_new = pltpu.make_async_copy(new_hbm, new_ref, local_sem.at[2])
    own_new.start()
    scalars = [
        pltpu.make_async_copy(lengths_hbm, lengths_ref, local_sem.at[3]),
        pltpu.make_async_copy(cache_len_hbm, cache_len_ref, local_sem.at[4]),
        pltpu.make_async_copy(slots_hbm, slots_ref, local_sem.at[5]),
    ]
    for c in scalars:
        c.start()

    def cache_copy(g):
        rows = pl.ds(g * 4, 4)
        return pltpu.make_async_copy(cache_ref.at[rows], cacheb.at[rows], cache_sem.at[g])

    @pl.when(is_dec)
    def _():
        for g in range(8):
            cache_copy(g).start()

    barrier = pltpu.get_barrier_semaphore()
    peers = [(0, dz) for dz in (1, 2, 4, 6, 7)] + [(1, 0), (2, 0), (3, 0)]
    for dy, dz in peers:
        pl.semaphore_signal(barrier, inc=1, device_id=dev(dy, dz), device_id_type=MESH)
    def clear(b, _):
        rows = pl.ds(pl.multiple_of(b * D, D), D)
        acc[rows, :] = jnp.zeros((D, D), F32)
        l[rows, :] = jnp.zeros((D, D), F32)
        m[rows, :] = jnp.full((D, D), NEG, F32)
        return 0

    lax.fori_loop(0, 20, clear, 0)

    own_kv.wait()
    own_new.wait()
    own_q.wait()
    for c in scalars:
        c.wait()
    pl.semaphore_wait(barrier, len(peers))

    own_stretch = pl.ds(pl.multiple_of(2 * 1024 + y * 128, 128), 128)
    slot = kvb.at[own_stretch]
    stretch_y = [remote(slot, slot, str_send.at[i], str_recv.at[i], dy, 0) for i, dy in enumerate((1, 3, 2))]
    stretch_z = remote(slot, slot, str_send.at[3], str_recv.at[3], 0, 1)
    def part(piece, h):
        return kvb.at[pl.ds((0, 1024, 2560, 3584)[piece] + h * half, half)]

    kv_copies = [
        remote(part(0, 0), part(1, 0), kv_send.at[0], kv_recv.at[0], 1, 0),
        remote(part(0, 1), part(1, 1), kv_send.at[1], kv_recv.at[1], 3, 0),
        remote(part(0, 1), part(2, 0), kv_send.at[2], kv_recv.at[2], 1, 0),
        remote(part(0, 0), part(2, 1), kv_send.at[3], kv_recv.at[3], 3, 0),
        remote(part(1, 0), part(3, 0), kv_send.at[4], kv_recv.at[4], 1, 0),
        remote(part(1, 1), part(3, 1), kv_send.at[5], kv_recv.at[5], 3, 0),
    ]
    home_q, near_q = qall.at[pl.ds(0, 1024)], qall.at[pl.ds(1024, 1024)]
    far_q = qall.at[pl.ds(2048, half)]
    q_copies = [
        remote(home_q, near_q, q_send.at[0], q_recv.at[0], 0, -1),
        remote(home_q, near_q, q_send.at[1], q_recv.at[0], 0, 2),
    ]
    far_q_pre = remote(qall.at[pl.ds(1024 + half, half)], far_q, q_send.at[2], q_recv.at[1], 0, 2)
    far_q_dec = remote(qall.at[pl.ds(1024, half)], far_q, q_send.at[2], q_recv.at[1], 0, -2)
    p_copies = [
        remote(pqall.at[0], pqall.at[d], p_send.at[d - 1], p_recv.at[d - 1], 0, 2 * d) for d in (1, 2, 3)
    ]
    p_back = []
    for d in (1, 2, 3):
        p_back.append(remote(pob.at[d], pback.at[d], pb_send.at[d - 1, 0], pb_recv.at[d - 1, 0], 0, -2 * d))
        p_back.append(remote(pls.at[d], plback.at[d], pb_send.at[d - 1, 1], pb_recv.at[d - 1, 1], 0, -2 * d))

    @pl.when(is_pre)
    def _():
        kvb[own_stretch, :] = new_ref[...]
        stretch_z.start()
        for c in stretch_y:
            c.start()

    for c in kv_copies[:4]:
        c.start()

    @pl.when(is_pre)
    def _():
        for c in q_copies:
            c.start()

    def block(row0, i):
        return pl.ds(pl.multiple_of(row0 + i * RB, RB), RB)

    def scores(b, k0, span, masked, s, mx):
        rows = block(0, b)
        x = dot(qall[rows, :], kvb[pl.ds(k0, span), :D], NT)
        s[:, :span] = x
        if masked is None:
            top = jnp.max(x, axis=1, keepdims=True)
        else:
            begin, place = stretch_range(b)
            keys = lax.broadcasted_iota(jnp.int32, (RB, half), 1) + zh * half
            y0 = jnp.where((keys >= begin) & (keys <= place), x[:, masked : masked + half], NEG)
            s[:, masked : masked + half] = y0
            top = jnp.maximum(
                jnp.max(x[:, :masked], axis=1, keepdims=True), jnp.max(y0, axis=1, keepdims=True)
            )
            if masked + half < span:
                top = jnp.maximum(top, jnp.max(x[:, masked + half :], axis=1, keepdims=True))
        mx[...] = jnp.broadcast_to(top * SCALE, mx.shape)

    def absorb(b, k0, span, s, mx):
        rows = block(0, b)
        old = m[rows, :]
        new = jnp.maximum(old, mx[...])
        shrink = jnp.exp2(old - new)
        m[rows, :] = new
        p = jnp.exp2(s[:, :span] * SCALE - new[:, :1]).astype(BF16)
        r = dot(p, with_ones(kvb[pl.ds(k0, span), D:]), NN)
        l[rows, :] = l[rows, :] * shrink + r[:, D:]
        acc[rows, :] = acc[rows, :] * shrink + r[:, :D]

    def attend(b0, n, k0, span, masked=None):
        scores(b0, k0, span, masked, sa, ma)

        def pair(j, _):
            b = b0 + 2 * j
            scores(b + 1, k0, span, masked, sb, mb)
            absorb(b, k0, span, sa, ma)
            scores(jnp.minimum(b + 2, b0 + n - 1), k0, span, masked, sa, ma)
            absorb(b + 1, k0, span, sb, mb)
            return 0

        lax.fori_loop(0, n // 2, pair, 0)

    def weigh(stats, values):
        top = functools.reduce(jnp.maximum, stats)
        weights = [jnp.exp2(x - top) for x in stats]
        total = functools.reduce(jnp.add, weights)
        mixed = functools.reduce(jnp.add, [w * v for w, v in zip(weights, values)])
        return mixed / total, top + jnp.log2(total)

    ends = []
    running = jnp.int32(0)
    for p in range(8):
        running = running + lengths_ref[p]
        ends.append(running)
    starts = [jnp.int32(0)] + ends[:-1]

    def small(qv, kv_value, mask, rows, m_ref, l_ref, acc_ref):
        s = jnp.where(mask, dot(qv, kv_value[:, :D], NT) * SCALE, NEG)
        old = m_ref[rows, :]
        new = jnp.maximum(old, jnp.max(s, axis=1, keepdims=True))
        shrink = jnp.exp2(old - new)
        p = jnp.exp2(s - new[:, :1]).astype(BF16)
        r = dot(p, with_ones(kv_value[:, D:]), NN)
        m_ref[rows, :] = new
        l_ref[rows, :] = l_ref[rows, :] * shrink + r[:, D:]
        acc_ref[rows, :] = acc_ref[rows, :] * shrink + r[:, :D]

    def stretch_range(i):
        index = lax.broadcasted_iota(jnp.int32, (RB, 1), 0) + i * RB
        own = i < 4
        near = i < 8
        home_zh = jnp.where(own, zh, jnp.where(near, zh + jnp.where(is_pre, 3, 1), zh + 2))
        home_zh = lax.rem(home_zh, 4)
        index = index - jnp.where(own, 0, jnp.where(near, 1024, jnp.where(is_pre, 2048 - half, 2048)))
        place = (home_zh * 4 + y) * 128 + (index // 32) * 4 + lax.rem(index, 4)
        begin = jnp.zeros_like(place)
        for e in ends[:-1]:
            begin = jnp.where(place >= e, e, begin)
        return begin, place

    first_row = seq * 32

    def fresh_block(i, _):
        rows = block(0, i)
        index = lax.broadcasted_iota(jnp.int32, (RB, D), 0) + i * RB
        key = lax.broadcasted_iota(jnp.int32, (RB, D), 1)
        mask = (key // 4 == index // 32) & (lax.rem(key, 4) <= lax.rem(index, 4))
        small(qall[rows, :], new_ref[...], mask, rows, m, l, acc)
        return 0

    def cache_rows(g, _):
        for u in range(4):
            r = g * 4 + u
            rows = pl.ds(pl.multiple_of(r * 32, 32), 32)
            length = cache_len_ref[first_row + r]
            mask = lax.broadcasted_iota(jnp.int32, (32, half), 1) < length
            small(qall[rows, :], cacheb[r], mask, rows, m, l, acc)
        return 0

    def decode_first():
        owner = lax.broadcasted_iota(jnp.int32, (256, 1), 0) // 32
        target = lax.rem(lax.broadcasted_iota(jnp.int32, (256, 1), 0), 32)
        for p in range(8):
            target = jnp.where(owner == p, target + (slots_ref[p] - first_row) * 32, target)
        chosen = lax.broadcasted_iota(jnp.int32, (256, 1024), 1) == target
        chosen = jnp.where(chosen, 1.0, 0.0).astype(BF16)
        pqall[0] = dot(chosen, qall[pl.ds(0, 1024), :], NN).astype(BF16)
        for c in p_copies:
            c.start()
        lax.fori_loop(0, 1024 // RB, fresh_block, 0)
        for g in range(4):
            cache_copy(g).wait()
        lax.fori_loop(0, 4, cache_rows, 0)
        stretch_z.wait_recv()
        for c in stretch_y:
            c.start()
        for g in range(4, 8):
            cache_copy(g).wait()
        lax.fori_loop(4, 8, cache_rows, 0)

    def prompt_part():
        for c in p_copies:
            c.wait_recv()
        pacc[...] = jnp.zeros_like(pacc)
        psum[...] = jnp.zeros_like(psum)
        pm[...] = jnp.full_like(pm, NEG)
        owner = lax.broadcasted_iota(jnp.int32, (256, 1), 0) // 32
        low = jnp.zeros_like(owner)
        high = jnp.zeros_like(owner)
        for p in range(8):
            low = jnp.where(owner == p, starts[p], low)
            high = jnp.where(owner == p, ends[p], high)
        keys = lax.broadcasted_iota(jnp.int32, (256, half), 1) + zh * half
        mask = (keys >= low) & (keys < high)

        def one(d, _):
            rows = block(0, d)
            small(pqall[d], kvb[pl.ds(2048, half), :], mask, rows, pm, psum, pacc)
            total = psum[rows, :]
            pob[d] = (pacc[rows, :] / total).astype(BF16)
            stat = pm[rows, :] + jnp.log2(total)
            pls[d] = jnp.zeros((8, D), F32)
            pls[d, pl.ds(0, 1), :] = jnp.transpose(stat[:D])[:1]
            pls[d, pl.ds(1, 1), :] = jnp.transpose(stat[D:])[:1]
            return 0

        lax.fori_loop(0, 4, one, 0)
        for c in p_back:
            c.start()

    def decode_last():
        for c in p_back:
            c.wait_recv()
        pback[0] = pob[0]
        plback[0] = pls[0]
        for b in range(2):
            rows = pl.ds(b * D, D)
            mixed, stat = weigh(
                [column(plback[d, pl.ds(b, 1), :]) for d in range(4)],
                [pback[d, rows, :].astype(F32) for d in range(4)],
            )
            pm[rows, :] = stat
            pacc[rows, :] = mixed

        def merge(r, _):
            rows = pl.ds(pl.multiple_of(r * 32, 32), 32)
            other = jnp.full((32, D), NEG, F32)
            value = jnp.zeros((32, D), F32)
            for p in range(8):
                theirs = pl.ds(p * 32, 32)
                hit = jnp.full((32, D), slots_ref[p] - first_row - r, jnp.int32) == 0
                other = jnp.where(hit, pm[theirs, :], other)
                value = jnp.where(hit, pacc[theirs, :], value)
            old = m[rows, :]
            new = jnp.maximum(old, other)
            w0 = jnp.exp2(old - new)
            w1 = jnp.exp2(other - new)
            mixed = acc[rows, :] * w0 + value * w1
            out_ref[rows, :] = (mixed / (l[rows, :] * w0 + w1)).astype(BF16)
            return 0

        lax.fori_loop(0, 32, merge, 0)

    far_o = ob.at[pl.ds(1024, half)]
    far_pre = [
        remote(far_o, rof, o_send.at[0], o_recv.at[0], 0, -2),
        remote(ls.at[2], rlf, l_send.at[0], l_recv.at[0], 0, -2),
    ]
    far_dec = [
        remote(far_o, rof, o_send.at[0], o_recv.at[0], 0, 2),
        remote(ls.at[2], rlf, l_send.at[0], l_recv.at[0], 0, 2),
    ]
    near_pre, near_dec = [], []
    for h in range(2):
        rows = pl.ds(h * half, half)
        near_pre.append([
            remote(ob.at[rows], ro.at[1, rows], o_send.at[1 + h], o_recv.at[3 + h], 0, -2),
            remote(ls.at[h], rl.at[1, h], l_send.at[1 + h], l_recv.at[3 + h], 0, -2),
        ])
        near_dec.append([
            remote(ob.at[rows], ro.at[0, rows], o_send.at[1 + h], o_recv.at[1 + h], 0, 1),
            remote(ls.at[h], rl.at[0, h], l_send.at[1 + h], l_recv.at[1 + h], 0, 1),
        ])

    def start_all(pre, dec):
        @pl.when(is_pre)
        def _():
            for c in pre:
                c.start()

        @pl.when(is_dec)
        def _():
            for c in dec:
                c.start()

    def finish_block(b, _):
        rows = pl.ds(pl.multiple_of(1024 + b * D, D), D)
        total = l[rows, :]
        ob[pl.ds(pl.multiple_of(b * D, D), D), :] = (acc[rows, :] / total).astype(BF16)
        stat = jnp.transpose(m[rows, :] + jnp.log2(total))
        ls[b // 4, pl.ds(lax.rem(b, 4), 1), :] = stat[:1, :]
        return 0

    def merge_block(b, _):
        rows = pl.ds(pl.multiple_of(1024 + b * D, D), D)
        theirs = lax.rem(b, 4)
        total = l[rows, :]
        mixed, stat = weigh(
            [m[rows, :] + jnp.log2(total), column(rlf[pl.ds(theirs, 1), :])],
            [acc[rows, :] / total, rof[pl.ds(pl.multiple_of(theirs * D, D), D), :].astype(F32)],
        )
        ob[pl.ds(pl.multiple_of(b * D, D), D), :] = mixed.astype(BF16)
        ls[b // 4, pl.ds(theirs, 1), :] = jnp.transpose(stat)[:1, :]
        return 0

    def send_far():
        ls[...] = jnp.zeros_like(ls)
        lax.fori_loop(8, 12, finish_block, 0)
        start_all(far_pre, far_dec)

    def send_near():
        first_block = jnp.where(is_pre, 0, 4)
        lax.fori_loop(first_block, first_block + 4, finish_block, 0)
        start_all(near_pre[0], near_dec[1])

    def send_merged():
        for c in far_pre:
            c.wait_recv()
        first_block = jnp.where(is_pre, 4, 0)
        lax.fori_loop(first_block, first_block + 4, merge_block, 0)
        start_all(near_pre[1], near_dec[0])

    def combine():
        for c in near_dec[1] + near_pre[0] + near_dec[0] + near_pre[1]:
            c.wait_recv()

        def one(b, _):
            rows = pl.ds(pl.multiple_of(b * D, D), D)
            total = l[rows, :]
            stats = [m[rows, :] + jnp.log2(total)]
            values = [acc[rows, :] / total]
            for i in range(2):
                stats.append(column(rl[i, b // 4, pl.ds(lax.rem(b, 4), 1), :]))
                values.append(ro[i, rows, :].astype(F32))
            mixed, _ = weigh(stats, values)
            out_ref[rows, :] = mixed.astype(BF16)
            return 0

        lax.fori_loop(0, 8, one, 0)

    @pl.when(is_pre)
    def _():
        attend(0, 4, 0, 1024)

    @pl.when(is_dec)
    def _():
        decode_first()

    for c in kv_copies[:2]:
        c.wait_recv()
    for c in kv_copies[4:]:
        c.start()
    q_copies[0].wait_recv()
    start_all([far_q_pre], [far_q_dec])
    for c in stretch_y:
        c.wait_recv()

    def wide(i, _):
        @pl.when(i == 1)
        def _():
            far_q_pre.wait_recv()

        attend(4 + 4 * i, 4 - 2 * i, 0, 2560, 2048)
        return 0

    lax.fori_loop(0, 2, wide, 0)

    @pl.when(is_dec)
    def _():
        prompt_part()

    def narrow(i, _):
        @pl.when(i == 0)
        def _():
            for c in kv_copies[2:4]:
                c.wait_recv()

        @pl.when(i == 1)
        def _():
            for c in kv_copies[4:]:
                c.wait_recv()

        attend(
            jnp.where(i == 1, 8, 4),
            jnp.where(i == 0, 6, jnp.where(i == 1, 2, 4)),
            pl.multiple_of(jnp.where(i == 0, 2560, 3584), half),
            1024,
        )

        @pl.when(i == 1)
        def _():
            send_far()

        return 0

    lax.fori_loop(0, 3, narrow, 0)
    send_near()

    def rest(i, _):
        @pl.when(is_pre)
        def _():
            attend(2 * i, 2, 1024, 3584, 1024)

        @pl.when(i == 0)
        def _():
            send_merged()

        return 0

    lax.fori_loop(0, 2, rest, 0)

    @pl.when(is_pre)
    def _():
        combine()

    @pl.when(is_dec)
    def _():
        decode_last()

    for c in kv_copies + stretch_y + [far_q_pre] + far_pre + near_pre[0] + near_pre[1]:
        c.wait_send()

    @pl.when(is_pre)
    def _():
        for c in [stretch_z] + q_copies:
            c.wait_send()

    @pl.when(is_dec)
    def _():
        for c in p_copies + p_back:
            c.wait_send()


def body(queries, new_kv, prefix_kv, cache_kv, prompt_lengths, cache_lengths, prompt_slots):
    q = queries.reshape(32, 4, 8, D).transpose(0, 2, 1, 3).reshape(1024, D)
    new = new_kv.reshape(128, 2 * D)
    prefix = prefix_kv.reshape(1024, 2 * D)
    cache = cache_kv.reshape(32, 512, 2 * D)
    vmem = pl.BlockSpec(memory_space=pltpu.VMEM)
    hbm = pl.BlockSpec(memory_space=pl.ANY)
    dma = pltpu.SemaphoreType.DMA
    out = pl.pallas_call(
        kernel,
        out_shape=jax.ShapeDtypeStruct((1024, D), BF16),
        in_specs=[hbm] * 7,
        out_specs=vmem,
        scratch_shapes=[
            pltpu.VMEM((4608, 2 * D), BF16),
            pltpu.VMEM((2560, D), BF16),
            pltpu.VMEM((2560, D), F32),
            pltpu.VMEM((2560, D), F32),
            pltpu.VMEM((2560, D), F32),
            pltpu.VMEM((1536, D), BF16),
            pltpu.VMEM((3, 8, D), F32),
            pltpu.VMEM((2, 1024, D), BF16),
            pltpu.VMEM((2, 2, 8, D), F32),
            pltpu.VMEM((512, D), BF16),
            pltpu.VMEM((8, D), F32),
            pltpu.VMEM((32, 512, 2 * D), BF16),
            pltpu.VMEM((RB, 3584), F32),
            pltpu.VMEM((RB, 3584), F32),
            pltpu.VMEM((RB, D), F32),
            pltpu.VMEM((RB, D), F32),
            pltpu.VMEM((4, 256, D), BF16),
            pltpu.VMEM((1024, D), F32),
            pltpu.VMEM((1024, D), F32),
            pltpu.VMEM((1024, D), F32),
            pltpu.VMEM((4, 256, D), BF16),
            pltpu.VMEM((4, 8, D), F32),
            pltpu.VMEM((4, 256, D), BF16),
            pltpu.VMEM((4, 8, D), F32),
            pltpu.VMEM((128, 2 * D), BF16),
            pltpu.SMEM((8,), jnp.int32),
            pltpu.SMEM((512,), jnp.int32),
            pltpu.SMEM((8,), jnp.int32),
            dma((6,)), dma((8,)), dma((6,)), dma((6,)), dma((3,)), dma((2,)),
            dma((4,)), dma((4,)), dma((3,)), dma((3,)), dma((3, 2)), dma((3, 2)),
            dma((3,)), dma((5,)), dma((3,)), dma((5,)),
        ],
        compiler_params=pltpu.CompilerParams(
            collective_id=0, has_side_effects=True, vmem_limit_bytes=62 * 2**20
        ),
        cost_estimate=pl.CostEstimate(flops=10**10, bytes_accessed=10**7, transcendentals=10**7),
    )(prompt_lengths, cache_lengths, prompt_slots, q, new, prefix, cache)
    return out.reshape(32, 8, 4, D).transpose(0, 2, 1, 3).reshape(1, 128, 1024)


def solution(mesh):
    return jax.shard_map(
        body,
        mesh=mesh,
        in_specs=(
            P("role", "seq", "tensor"),
            P("role", "seq", "tensor", None),
            P("seq", "tensor", None),
            P("seq", None, "tensor", None),
            P(),
            P(),
            P(),
        ),
        out_specs=P("role", "seq", "tensor"),
        check_vma=False,
    )
```

```python
import functools
import math

import jax
import jax.numpy as jnp
from jax import lax
from jax.experimental import pallas as pl
from jax.experimental.pallas import tpu as pltpu
from jax.sharding import PartitionSpec as P

MESH = pl.DeviceIdType.MESH
NEG = -1e30
D = 128
SCALE = math.log2(math.e) / math.sqrt(D)
RB = 256
NT = (((1,), (1,)), ((), ()))
NN = (((1,), (0,)), ((), ()))
F32 = jnp.float32
BF16 = jnp.bfloat16


def dot(a, b, dims):
    return lax.dot_general(a, b, dims, preferred_element_type=F32)


def with_ones(v):
    return jnp.concatenate([v, jnp.ones_like(v)], axis=1)


def column(row):
    return jnp.transpose(jnp.broadcast_to(row, (D, D)))


def kernel(
    lengths_hbm, cache_len_hbm, slots_hbm, q_ref, new_hbm, prefix_ref, cache_ref,
    out_ref,
    kvb, qall, acc, m, l, ob, ls, ro, rl, rof, rlf, cacheb, sa, sb, ma, mb,
    pqall, pacc, pm, psum, pob, pls, pback, plback, new_ref, lengths_ref, cache_len_ref, slots_ref,
    local_sem, cache_sem, kv_send, kv_recv, q_send, q_recv, str_send, str_recv,
    p_send, p_recv, pb_send, pb_recv, o_send, o_recv, l_send, l_recv,
):
    role = lax.axis_index("role")
    seq = lax.axis_index("seq")
    tensor = lax.axis_index("tensor")
    zh, y = seq // 4, lax.rem(seq, 4)
    z = zh * 2 + role

    def dev(dy, dz):
        yy = lax.rem(y + dy + 8, 4)
        zz = lax.rem(z + dz + 8, 8)
        return (lax.rem(zz, 2), (zz // 2) * 4 + yy, tensor)

    def remote(src, dst, ss, rs, dy, dz):
        return pltpu.make_async_remote_copy(
            src_ref=src, dst_ref=dst, send_sem=ss, recv_sem=rs,
            device_id=dev(dy, dz), device_id_type=MESH,
        )

    is_pre = role == 0
    is_dec = role == 1
    half = 512

    own_kv = pltpu.make_async_copy(prefix_ref, kvb.at[pl.ds(0, 1024)], local_sem.at[0])
    own_kv.start()
    own_q = pltpu.make_async_copy(q_ref, qall.at[pl.ds(0, 1024)], local_sem.at[1])
    own_q.start()
    own_new = pltpu.make_async_copy(new_hbm, new_ref, local_sem.at[2])
    own_new.start()
    scalars = [
        pltpu.make_async_copy(lengths_hbm, lengths_ref, local_sem.at[3]),
        pltpu.make_async_copy(cache_len_hbm, cache_len_ref, local_sem.at[4]),
        pltpu.make_async_copy(slots_hbm, slots_ref, local_sem.at[5]),
    ]
    for c in scalars:
        c.start()

    def cache_copy(g):
        rows = pl.ds(g * 4, 4)
        return pltpu.make_async_copy(cache_ref.at[rows], cacheb.at[rows], cache_sem.at[g])

    barrier = pltpu.get_barrier_semaphore()
    peers = [(0, dz) for dz in (1, 2, 4, 6, 7)] + [(1, 0), (2, 0), (3, 0)]
    for dy, dz in peers:
        pl.semaphore_signal(barrier, inc=1, device_id=dev(dy, dz), device_id_type=MESH)
    def clear(b, _):
        rows = pl.ds(pl.multiple_of(b * D, D), D)
        acc[rows, :] = jnp.zeros((D, D), F32)
        l[rows, :] = jnp.zeros((D, D), F32)
        m[rows, :] = jnp.full((D, D), NEG, F32)
        return 0

    lax.fori_loop(0, 20, clear, 0)

    own_kv.wait()
    own_new.wait()
    own_q.wait()
    for c in scalars:
        c.wait()
    pl.semaphore_wait(barrier, len(peers))

    own_stretch = pl.ds(pl.multiple_of(2 * 1024 + y * 128, 128), 128)
    slot = kvb.at[own_stretch]
    stretch_y = [remote(slot, slot, str_send.at[i], str_recv.at[i], dy, 0) for i, dy in enumerate((1, 3, 2))]
    stretch_z = remote(slot, slot, str_send.at[3], str_recv.at[3], 0, 1)
    def part(piece, h):
        return kvb.at[pl.ds((0, 1024, 2560, 3584)[piece] + h * half, half)]

    kv_copies = [
        remote(part(0, 0), part(1, 0), kv_send.at[0], kv_recv.at[0], 1, 0),
        remote(part(0, 1), part(1, 1), kv_send.at[1], kv_recv.at[1], 3, 0),
        remote(part(0, 1), part(2, 0), kv_send.at[2], kv_recv.at[2], 1, 0),
        remote(part(0, 0), part(2, 1), kv_send.at[3], kv_recv.at[3], 3, 0),
        remote(part(1, 0), part(3, 0), kv_send.at[4], kv_recv.at[4], 1, 0),
        remote(part(1, 1), part(3, 1), kv_send.at[5], kv_recv.at[5], 3, 0),
    ]
    home_q, near_q = qall.at[pl.ds(0, 1024)], qall.at[pl.ds(1024, 1024)]
    far_q = qall.at[pl.ds(2048, half)]
    q_copies = [
        remote(home_q, near_q, q_send.at[0], q_recv.at[0], 0, -1),
        remote(home_q, near_q, q_send.at[1], q_recv.at[0], 0, 2),
    ]
    far_q_pre = remote(qall.at[pl.ds(1024 + half, half)], far_q, q_send.at[2], q_recv.at[1], 0, 2)
    far_q_dec = remote(qall.at[pl.ds(1024, half)], far_q, q_send.at[2], q_recv.at[1], 0, -2)
    p_copies = [
        remote(pqall.at[0], pqall.at[d], p_send.at[d - 1], p_recv.at[d - 1], 0, 2 * d) for d in (1, 2, 3)
    ]
    p_back = []
    for d in (1, 2, 3):
        p_back.append(remote(pob.at[d], pback.at[d], pb_send.at[d - 1, 0], pb_recv.at[d - 1, 0], 0, -2 * d))
        p_back.append(remote(pls.at[d], plback.at[d], pb_send.at[d - 1, 1], pb_recv.at[d - 1, 1], 0, -2 * d))

    @pl.when(is_pre)
    def _():
        kvb[own_stretch, :] = new_ref[...]
        stretch_z.start()

    for c in kv_copies[:2]:
        c.start()

    @pl.when(is_pre)
    def _():
        for c in q_copies:
            c.start()

    @pl.when(is_dec)
    def _():
        for g in range(8):
            cache_copy(g).start()

    def block(row0, i):
        return pl.ds(pl.multiple_of(row0 + i * RB, RB), RB)

    def scores(b, k0, span, masked, s, mx):
        rows = block(0, b)
        x = dot(qall[rows, :], kvb[pl.ds(k0, span), :D], NT)
        s[:, :span] = x
        if masked is None:
            top = jnp.max(x, axis=1, keepdims=True)
        else:
            begin, place = stretch_range(b)
            keys = lax.broadcasted_iota(jnp.int32, (RB, half), 1) + zh * half
            y0 = jnp.where((keys >= begin) & (keys <= place), x[:, masked : masked + half], NEG)
            s[:, masked : masked + half] = y0
            top = jnp.max(y0, axis=1, keepdims=True)
            if masked:
                top = jnp.maximum(top, jnp.max(x[:, :masked], axis=1, keepdims=True))
            if masked + half < span:
                top = jnp.maximum(top, jnp.max(x[:, masked + half :], axis=1, keepdims=True))
        mx[...] = jnp.broadcast_to(top * SCALE, mx.shape)

    def absorb(b, k0, span, s, mx):
        rows = block(0, b)
        old = m[rows, :]
        new = jnp.maximum(old, mx[...])
        shrink = jnp.exp2(old - new)
        m[rows, :] = new
        p = jnp.exp2(s[:, :span] * SCALE - new[:, :1]).astype(BF16)
        r = dot(p, with_ones(kvb[pl.ds(k0, span), D:]), NN)
        l[rows, :] = l[rows, :] * shrink + r[:, D:]
        acc[rows, :] = acc[rows, :] * shrink + r[:, :D]

    def attend(b0, n, k0, span, masked=None):
        scores(b0, k0, span, masked, sa, ma)

        def pair(j, _):
            b = b0 + 2 * j
            scores(b + 1, k0, span, masked, sb, mb)
            absorb(b, k0, span, sa, ma)
            scores(jnp.minimum(b + 2, b0 + n - 1), k0, span, masked, sa, ma)
            absorb(b + 1, k0, span, sb, mb)
            return 0

        lax.fori_loop(0, n // 2, pair, 0)

    def weigh(stats, values):
        top = functools.reduce(jnp.maximum, stats)
        weights = [jnp.exp2(x - top) for x in stats]
        total = functools.reduce(jnp.add, weights)
        mixed = functools.reduce(jnp.add, [w * v for w, v in zip(weights, values)])
        return mixed / total, top + jnp.log2(total)

    ends = []
    running = jnp.int32(0)
    for p in range(8):
        running = running + lengths_ref[p]
        ends.append(running)
    starts = [jnp.int32(0)] + ends[:-1]

    def small(qv, kv_value, mask, rows, m_ref, l_ref, acc_ref):
        s = jnp.where(mask, dot(qv, kv_value[:, :D], NT) * SCALE, NEG)
        old = m_ref[rows, :]
        new = jnp.maximum(old, jnp.max(s, axis=1, keepdims=True))
        shrink = jnp.exp2(old - new)
        p = jnp.exp2(s - new[:, :1]).astype(BF16)
        r = dot(p, with_ones(kv_value[:, D:]), NN)
        m_ref[rows, :] = new
        l_ref[rows, :] = l_ref[rows, :] * shrink + r[:, D:]
        acc_ref[rows, :] = acc_ref[rows, :] * shrink + r[:, :D]

    def stretch_range(i):
        index = lax.broadcasted_iota(jnp.int32, (RB, 1), 0) + i * RB
        own = i < 4
        near = i < 8
        home_zh = jnp.where(own, zh, jnp.where(near, zh + jnp.where(is_pre, 3, 1), zh + 2))
        home_zh = lax.rem(home_zh, 4)
        index = index - jnp.where(own, 0, jnp.where(near, 1024, jnp.where(is_pre, 2048 - half, 2048)))
        place = (home_zh * 4 + y) * 128 + (index // 32) * 4 + lax.rem(index, 4)
        begin = jnp.zeros_like(place)
        for e in ends[:-1]:
            begin = jnp.where(place >= e, e, begin)
        return begin, place

    first_row = seq * 32

    def fresh_block(i, _):
        rows = block(0, i)
        index = lax.broadcasted_iota(jnp.int32, (RB, D), 0) + i * RB
        key = lax.broadcasted_iota(jnp.int32, (RB, D), 1)
        mask = (key // 4 == index // 32) & (lax.rem(key, 4) <= lax.rem(index, 4))
        small(qall[rows, :], new_ref[...], mask, rows, m, l, acc)
        return 0

    def cache_rows(g, _):
        for u in range(4):
            r = g * 4 + u
            rows = pl.ds(pl.multiple_of(r * 32, 32), 32)
            length = cache_len_ref[first_row + r]
            mask = lax.broadcasted_iota(jnp.int32, (32, half), 1) < length
            small(qall[rows, :], cacheb[r], mask, rows, m, l, acc)
        return 0

    def second_copies():
        for c in kv_copies[:2]:
            c.wait_send()
        for c in stretch_y + kv_copies[2:4]:
            c.start()

    def decode_first():
        owner = lax.broadcasted_iota(jnp.int32, (256, 1), 0) // 32
        target = lax.rem(lax.broadcasted_iota(jnp.int32, (256, 1), 0), 32)
        for p in range(8):
            target = jnp.where(owner == p, target + (slots_ref[p] - first_row) * 32, target)
        chosen = lax.broadcasted_iota(jnp.int32, (256, 1024), 1) == target
        chosen = jnp.where(chosen, 1.0, 0.0).astype(BF16)
        pqall[0] = dot(chosen, qall[pl.ds(0, 1024), :], NN).astype(BF16)
        for c in p_copies:
            c.start()
        lax.fori_loop(0, 1024 // RB, fresh_block, 0)
        for g in range(4):
            cache_copy(g).wait()
        lax.fori_loop(0, 4, cache_rows, 0)
        stretch_z.wait_recv()
        second_copies()
        for g in range(4, 8):
            cache_copy(g).wait()
        lax.fori_loop(4, 8, cache_rows, 0)

    def prompt_part():
        for c in p_copies:
            c.wait_recv()
        pacc[...] = jnp.zeros_like(pacc)
        psum[...] = jnp.zeros_like(psum)
        pm[...] = jnp.full_like(pm, NEG)
        owner = lax.broadcasted_iota(jnp.int32, (256, 1), 0) // 32
        low = jnp.zeros_like(owner)
        high = jnp.zeros_like(owner)
        for p in range(8):
            low = jnp.where(owner == p, starts[p], low)
            high = jnp.where(owner == p, ends[p], high)
        keys = lax.broadcasted_iota(jnp.int32, (256, half), 1) + zh * half
        mask = (keys >= low) & (keys < high)

        def one(d, _):
            rows = block(0, d)
            small(pqall[d], kvb[pl.ds(2048, half), :], mask, rows, pm, psum, pacc)
            total = psum[rows, :]
            pob[d] = (pacc[rows, :] / total).astype(BF16)
            stat = pm[rows, :] + jnp.log2(total)
            pls[d] = jnp.zeros((8, D), F32)
            pls[d, pl.ds(0, 1), :] = jnp.transpose(stat[:D])[:1]
            pls[d, pl.ds(1, 1), :] = jnp.transpose(stat[D:])[:1]
            return 0

        lax.fori_loop(0, 4, one, 0)
        for c in p_back:
            c.start()

    def decode_last():
        for c in p_back:
            c.wait_recv()
        pback[0] = pob[0]
        plback[0] = pls[0]
        for b in range(2):
            rows = pl.ds(b * D, D)
            mixed, stat = weigh(
                [column(plback[d, pl.ds(b, 1), :]) for d in range(4)],
                [pback[d, rows, :].astype(F32) for d in range(4)],
            )
            pm[rows, :] = stat
            pacc[rows, :] = mixed

        def merge(r, _):
            rows = pl.ds(pl.multiple_of(r * 32, 32), 32)
            other = jnp.full((32, D), NEG, F32)
            value = jnp.zeros((32, D), F32)
            for p in range(8):
                theirs = pl.ds(p * 32, 32)
                hit = jnp.full((32, D), slots_ref[p] - first_row - r, jnp.int32) == 0
                other = jnp.where(hit, pm[theirs, :], other)
                value = jnp.where(hit, pacc[theirs, :], value)
            old = m[rows, :]
            new = jnp.maximum(old, other)
            w0 = jnp.exp2(old - new)
            w1 = jnp.exp2(other - new)
            mixed = acc[rows, :] * w0 + value * w1
            out_ref[rows, :] = (mixed / (l[rows, :] * w0 + w1)).astype(BF16)
            return 0

        lax.fori_loop(0, 32, merge, 0)

    far_o = ob.at[pl.ds(1024, half)]
    far_pre = [
        remote(far_o, rof, o_send.at[0], o_recv.at[0], 0, -2),
        remote(ls.at[2], rlf, l_send.at[0], l_recv.at[0], 0, -2),
    ]
    far_dec = [
        remote(far_o, rof, o_send.at[0], o_recv.at[0], 0, 2),
        remote(ls.at[2], rlf, l_send.at[0], l_recv.at[0], 0, 2),
    ]
    near_pre, near_dec = [], []
    for h in range(2):
        rows = pl.ds(h * half, half)
        near_pre.append([
            remote(ob.at[rows], ro.at[1, rows], o_send.at[1 + h], o_recv.at[3 + h], 0, -2),
            remote(ls.at[h], rl.at[1, h], l_send.at[1 + h], l_recv.at[3 + h], 0, -2),
        ])
        near_dec.append([
            remote(ob.at[rows], ro.at[0, rows], o_send.at[1 + h], o_recv.at[1 + h], 0, 1),
            remote(ls.at[h], rl.at[0, h], l_send.at[1 + h], l_recv.at[1 + h], 0, 1),
        ])

    def start_all(pre, dec):
        @pl.when(is_pre)
        def _():
            for c in pre:
                c.start()

        @pl.when(is_dec)
        def _():
            for c in dec:
                c.start()

    def finish_block(b, _):
        rows = pl.ds(pl.multiple_of(1024 + b * D, D), D)
        total = l[rows, :]
        ob[pl.ds(pl.multiple_of(b * D, D), D), :] = (acc[rows, :] / total).astype(BF16)
        stat = jnp.transpose(m[rows, :] + jnp.log2(total))
        ls[b // 4, pl.ds(lax.rem(b, 4), 1), :] = stat[:1, :]
        return 0

    def merge_block(b, _):
        rows = pl.ds(pl.multiple_of(1024 + b * D, D), D)
        theirs = lax.rem(b, 4)
        total = l[rows, :]
        mixed, stat = weigh(
            [m[rows, :] + jnp.log2(total), column(rlf[pl.ds(theirs, 1), :])],
            [acc[rows, :] / total, rof[pl.ds(pl.multiple_of(theirs * D, D), D), :].astype(F32)],
        )
        ob[pl.ds(pl.multiple_of(b * D, D), D), :] = mixed.astype(BF16)
        ls[b // 4, pl.ds(theirs, 1), :] = jnp.transpose(stat)[:1, :]
        return 0

    def send_far():
        ls[...] = jnp.zeros_like(ls)
        lax.fori_loop(8, 12, finish_block, 0)
        start_all(far_pre, far_dec)

    def send_near():
        first_block = jnp.where(is_pre, 0, 4)
        lax.fori_loop(first_block, first_block + 4, finish_block, 0)
        start_all(near_pre[0], near_dec[1])

    def send_merged():
        for c in far_pre:
            c.wait_recv()
        first_block = jnp.where(is_pre, 4, 0)
        lax.fori_loop(first_block, first_block + 4, merge_block, 0)
        start_all(near_pre[1], near_dec[0])

    def combine():
        for c in near_dec[1] + near_pre[0] + near_dec[0] + near_pre[1]:
            c.wait_recv()

        def one(b, _):
            rows = pl.ds(pl.multiple_of(b * D, D), D)
            total = l[rows, :]
            stats = [m[rows, :] + jnp.log2(total)]
            values = [acc[rows, :] / total]
            for i in range(2):
                stats.append(column(rl[i, b // 4, pl.ds(lax.rem(b, 4), 1), :]))
                values.append(ro[i, rows, :].astype(F32))
            mixed, _ = weigh(stats, values)
            out_ref[rows, :] = mixed.astype(BF16)
            return 0

        lax.fori_loop(0, 8, one, 0)

    @pl.when(is_pre)
    def _():
        attend(0, 4, 0, 1024)
        second_copies()

    @pl.when(is_dec)
    def _():
        decode_first()

    for c in kv_copies[:2]:
        c.wait_recv()
    q_copies[0].wait_recv()
    start_all([far_q_pre], [far_q_dec])

    def wide(i, _):
        @pl.when(i == 1)
        def _():
            for c in kv_copies[4:]:
                c.start()
            far_q_pre.wait_recv()

        attend(4 + 4 * i, 4 - 2 * i, 0, 2048)
        return 0

    lax.fori_loop(0, 2, wide, 0)
    for c in stretch_y + kv_copies[2:4]:
        c.wait_recv()
    attend(4, 6, 2048, 1536, 0)
    for c in kv_copies[4:]:
        c.wait_recv()

    def narrow(i, _):
        attend(8 - 4 * i, 2 + 2 * i, 3584, 1024)

        @pl.when(i == 0)
        def _():
            send_far()

        return 0

    lax.fori_loop(0, 2, narrow, 0)
    send_near()

    @pl.when(is_dec)
    def _():
        prompt_part()

    def rest(i, _):
        @pl.when(is_pre)
        def _():
            attend(2 * i, 2, 1024, 3584, 1024)

        @pl.when(i == 0)
        def _():
            send_merged()

        return 0

    lax.fori_loop(0, 2, rest, 0)

    @pl.when(is_pre)
    def _():
        combine()

    @pl.when(is_dec)
    def _():
        decode_last()

    for c in kv_copies[2:] + stretch_y + [far_q_pre] + far_pre + near_pre[0] + near_pre[1]:
        c.wait_send()

    @pl.when(is_pre)
    def _():
        for c in [stretch_z] + q_copies:
            c.wait_send()

    @pl.when(is_dec)
    def _():
        for c in p_copies + p_back:
            c.wait_send()


def body(queries, new_kv, prefix_kv, cache_kv, prompt_lengths, cache_lengths, prompt_slots):
    q = queries.reshape(32, 4, 8, D).transpose(0, 2, 1, 3).reshape(1024, D)
    new = new_kv.reshape(128, 2 * D)
    prefix = prefix_kv.reshape(1024, 2 * D)
    cache = cache_kv.reshape(32, 512, 2 * D)
    vmem = pl.BlockSpec(memory_space=pltpu.VMEM)
    hbm = pl.BlockSpec(memory_space=pl.ANY)
    dma = pltpu.SemaphoreType.DMA
    out = pl.pallas_call(
        kernel,
        out_shape=jax.ShapeDtypeStruct((1024, D), BF16),
        in_specs=[hbm] * 7,
        out_specs=vmem,
        scratch_shapes=[
            pltpu.VMEM((4608, 2 * D), BF16),
            pltpu.VMEM((2560, D), BF16),
            pltpu.VMEM((2560, D), F32),
            pltpu.VMEM((2560, D), F32),
            pltpu.VMEM((2560, D), F32),
            pltpu.VMEM((1536, D), BF16),
            pltpu.VMEM((3, 8, D), F32),
            pltpu.VMEM((2, 1024, D), BF16),
            pltpu.VMEM((2, 2, 8, D), F32),
            pltpu.VMEM((512, D), BF16),
            pltpu.VMEM((8, D), F32),
            pltpu.VMEM((32, 512, 2 * D), BF16),
            pltpu.VMEM((RB, 3584), F32),
            pltpu.VMEM((RB, 3584), F32),
            pltpu.VMEM((RB, D), F32),
            pltpu.VMEM((RB, D), F32),
            pltpu.VMEM((4, 256, D), BF16),
            pltpu.VMEM((1024, D), F32),
            pltpu.VMEM((1024, D), F32),
            pltpu.VMEM((1024, D), F32),
            pltpu.VMEM((4, 256, D), BF16),
            pltpu.VMEM((4, 8, D), F32),
            pltpu.VMEM((4, 256, D), BF16),
            pltpu.VMEM((4, 8, D), F32),
            pltpu.VMEM((128, 2 * D), BF16),
            pltpu.SMEM((8,), jnp.int32),
            pltpu.SMEM((512,), jnp.int32),
            pltpu.SMEM((8,), jnp.int32),
            dma((6,)), dma((8,)), dma((6,)), dma((6,)), dma((3,)), dma((2,)),
            dma((4,)), dma((4,)), dma((3,)), dma((3,)), dma((3, 2)), dma((3, 2)),
            dma((3,)), dma((5,)), dma((3,)), dma((5,)),
        ],
        compiler_params=pltpu.CompilerParams(
            collective_id=0, has_side_effects=True, vmem_limit_bytes=62 * 2**20
        ),
        cost_estimate=pl.CostEstimate(flops=10**10, bytes_accessed=10**7, transcendentals=10**7),
    )(prompt_lengths, cache_lengths, prompt_slots, q, new, prefix, cache)
    return out.reshape(32, 8, 4, D).transpose(0, 2, 1, 3).reshape(1, 128, 1024)


def solution(mesh):
    return jax.shard_map(
        body,
        mesh=mesh,
        in_specs=(
            P("role", "seq", "tensor"),
            P("role", "seq", "tensor", None),
            P("seq", "tensor", None),
            P("seq", None, "tensor", None),
            P(),
            P(),
            P(),
        ),
        out_specs=P("role", "seq", "tensor"),
        check_vma=False,
    )
```

```python
import functools
import math

import jax
import jax.numpy as jnp
from jax import lax
from jax.experimental import pallas as pl
from jax.experimental.pallas import tpu as pltpu
from jax.sharding import PartitionSpec as P

MESH = pl.DeviceIdType.MESH
NEG = -1e30
D = 128
SCALE = math.log2(math.e) / math.sqrt(D)
RB = 256
NT = (((1,), (1,)), ((), ()))
NN = (((1,), (0,)), ((), ()))
F32 = jnp.float32
BF16 = jnp.bfloat16


def dot(a, b, dims):
    return lax.dot_general(a, b, dims, preferred_element_type=F32)


def with_ones(v):
    return jnp.concatenate([v, jnp.ones_like(v)], axis=1)


def column(row):
    return jnp.transpose(jnp.broadcast_to(row, (D, D)))


def kernel(
    lengths_hbm, cache_len_hbm, slots_hbm, q_ref, new_hbm, prefix_ref, cache_ref,
    out_ref,
    kvb, qall, acc, m, l, ob, ls, ro, rl, rof, rlf, cacheb, sa, sb, ma, mb,
    pqall, pacc, pm, psum, pob, pls, pback, plback, new_ref, lengths_ref, cache_len_ref, slots_ref,
    local_sem, cache_sem, kv_send, kv_recv, q_send, q_recv, str_send, str_recv,
    p_send, p_recv, pb_send, pb_recv, o_send, o_recv, l_send, l_recv,
):
    role = lax.axis_index("role")
    seq = lax.axis_index("seq")
    tensor = lax.axis_index("tensor")
    zh, y = seq // 4, lax.rem(seq, 4)
    z = zh * 2 + role

    def dev(dy, dz):
        yy = lax.rem(y + dy + 8, 4)
        zz = lax.rem(z + dz + 8, 8)
        return (lax.rem(zz, 2), (zz // 2) * 4 + yy, tensor)

    def remote(src, dst, ss, rs, dy, dz):
        return pltpu.make_async_remote_copy(
            src_ref=src, dst_ref=dst, send_sem=ss, recv_sem=rs,
            device_id=dev(dy, dz), device_id_type=MESH,
        )

    is_pre = role == 0
    is_dec = role == 1
    half = 512

    own_kv = pltpu.make_async_copy(prefix_ref, kvb.at[pl.ds(0, 1024)], local_sem.at[0])
    own_kv.start()
    own_q = pltpu.make_async_copy(q_ref, qall.at[pl.ds(0, 1024)], local_sem.at[1])
    own_q.start()
    own_new = pltpu.make_async_copy(new_hbm, new_ref, local_sem.at[2])
    own_new.start()
    scalars = [
        pltpu.make_async_copy(lengths_hbm, lengths_ref, local_sem.at[3]),
        pltpu.make_async_copy(cache_len_hbm, cache_len_ref, local_sem.at[4]),
        pltpu.make_async_copy(slots_hbm, slots_ref, local_sem.at[5]),
    ]
    for c in scalars:
        c.start()

    def cache_copy(g):
        rows = pl.ds(g * 4, 4)
        return pltpu.make_async_copy(cache_ref.at[rows], cacheb.at[rows], cache_sem.at[g])

    barrier = pltpu.get_barrier_semaphore()
    peers = [(0, dz) for dz in (1, 2, 4, 6, 7)] + [(1, 0), (2, 0), (3, 0)]
    for dy, dz in peers:
        pl.semaphore_signal(barrier, inc=1, device_id=dev(dy, dz), device_id_type=MESH)
    def clear(b, _):
        rows = pl.ds(pl.multiple_of(b * D, D), D)
        acc[rows, :] = jnp.zeros((D, D), F32)
        l[rows, :] = jnp.zeros((D, D), F32)
        m[rows, :] = jnp.full((D, D), NEG, F32)
        return 0

    lax.fori_loop(0, 20, clear, 0)

    own_kv.wait()
    own_new.wait()
    own_q.wait()
    for c in scalars:
        c.wait()
    pl.semaphore_wait(barrier, len(peers))

    own_stretch = pl.ds(pl.multiple_of(2 * 1024 + y * 128, 128), 128)
    slot = kvb.at[own_stretch]
    stretch_y = [remote(slot, slot, str_send.at[i], str_recv.at[i], dy, 0) for i, dy in enumerate((1, 3, 2))]
    stretch_z = remote(slot, slot, str_send.at[3], str_recv.at[3], 0, 1)
    def part(piece, h):
        return kvb.at[pl.ds((0, 1024, 2560, 3584)[piece] + h * half, half)]

    kv_copies = [
        remote(part(0, 0), part(1, 0), kv_send.at[0], kv_recv.at[0], 1, 0),
        remote(part(0, 1), part(1, 1), kv_send.at[1], kv_recv.at[1], 3, 0),
        remote(part(0, 1), part(2, 0), kv_send.at[2], kv_recv.at[2], 1, 0),
        remote(part(0, 0), part(2, 1), kv_send.at[3], kv_recv.at[3], 3, 0),
        remote(part(1, 0), part(3, 0), kv_send.at[4], kv_recv.at[4], 1, 0),
        remote(part(1, 1), part(3, 1), kv_send.at[5], kv_recv.at[5], 3, 0),
    ]
    home_q, near_q = qall.at[pl.ds(0, 1024)], qall.at[pl.ds(1024, 1024)]
    far_q = qall.at[pl.ds(2048, half)]
    q_copies = [
        remote(home_q, near_q, q_send.at[0], q_recv.at[0], 0, -1),
        remote(home_q, near_q, q_send.at[1], q_recv.at[0], 0, 2),
    ]
    far_q_pre = remote(qall.at[pl.ds(1024 + half, half)], far_q, q_send.at[2], q_recv.at[1], 0, 2)
    far_q_dec = remote(qall.at[pl.ds(1024, half)], far_q, q_send.at[2], q_recv.at[1], 0, -2)
    p_copies = [
        remote(pqall.at[0], pqall.at[d], p_send.at[d - 1], p_recv.at[d - 1], 0, 2 * d) for d in (1, 2, 3)
    ]
    p_back = []
    for d in (1, 2, 3):
        p_back.append(remote(pob.at[d], pback.at[d], pb_send.at[d - 1, 0], pb_recv.at[d - 1, 0], 0, -2 * d))
        p_back.append(remote(pls.at[d], plback.at[d], pb_send.at[d - 1, 1], pb_recv.at[d - 1, 1], 0, -2 * d))

    @pl.when(is_pre)
    def _():
        kvb[own_stretch, :] = new_ref[...]
        stretch_z.start()

    for c in kv_copies[:2]:
        c.start()

    @pl.when(is_pre)
    def _():
        for c in q_copies:
            c.start()

    @pl.when(is_dec)
    def _():
        for g in range(8):
            cache_copy(g).start()

    def block(row0, i):
        return pl.ds(pl.multiple_of(row0 + i * RB, RB), RB)

    def scores(b, k0, span, masked, s, mx):
        rows = block(0, b)
        x = dot(qall[rows, :], kvb[pl.ds(k0, span), :D], NT)
        s[:, :span] = x
        if masked is None:
            top = jnp.max(x, axis=1, keepdims=True)
        else:
            begin, place = stretch_range(b)
            keys = lax.broadcasted_iota(jnp.int32, (RB, half), 1) + zh * half
            y0 = jnp.where((keys >= begin) & (keys <= place), x[:, masked : masked + half], NEG)
            s[:, masked : masked + half] = y0
            top = jnp.max(y0, axis=1, keepdims=True)
            if masked:
                top = jnp.maximum(top, jnp.max(x[:, :masked], axis=1, keepdims=True))
            if masked + half < span:
                top = jnp.maximum(top, jnp.max(x[:, masked + half :], axis=1, keepdims=True))
        mx[...] = jnp.broadcast_to(top * SCALE, mx.shape)

    def absorb(b, k0, span, s, mx):
        rows = block(0, b)
        old = m[rows, :]
        new = jnp.maximum(old, mx[...])
        shrink = jnp.exp2(old - new)
        m[rows, :] = new
        p = jnp.exp2(s[:, :span] * SCALE - new[:, :1]).astype(BF16)
        r = dot(p, with_ones(kvb[pl.ds(k0, span), D:]), NN)
        l[rows, :] = l[rows, :] * shrink + r[:, D:]
        acc[rows, :] = acc[rows, :] * shrink + r[:, :D]

    def attend(b0, n, k0, span, masked=None):
        scores(b0, k0, span, masked, sa, ma)

        def pair(j, _):
            b = b0 + 2 * j
            scores(b + 1, k0, span, masked, sb, mb)
            absorb(b, k0, span, sa, ma)
            scores(jnp.minimum(b + 2, b0 + n - 1), k0, span, masked, sa, ma)
            absorb(b + 1, k0, span, sb, mb)
            return 0

        lax.fori_loop(0, n // 2, pair, 0)

    def weigh(stats, values):
        top = functools.reduce(jnp.maximum, stats)
        weights = [jnp.exp2(x - top) for x in stats]
        total = functools.reduce(jnp.add, weights)
        mixed = functools.reduce(jnp.add, [w * v for w, v in zip(weights, values)])
        return mixed / total, top + jnp.log2(total)

    ends = []
    running = jnp.int32(0)
    for p in range(8):
        running = running + lengths_ref[p]
        ends.append(running)
    starts = [jnp.int32(0)] + ends[:-1]

    def small(qv, kv_value, mask, rows, m_ref, l_ref, acc_ref):
        s = jnp.where(mask, dot(qv, kv_value[:, :D], NT) * SCALE, NEG)
        old = m_ref[rows, :]
        new = jnp.maximum(old, jnp.max(s, axis=1, keepdims=True))
        shrink = jnp.exp2(old - new)
        p = jnp.exp2(s - new[:, :1]).astype(BF16)
        r = dot(p, with_ones(kv_value[:, D:]), NN)
        m_ref[rows, :] = new
        l_ref[rows, :] = l_ref[rows, :] * shrink + r[:, D:]
        acc_ref[rows, :] = acc_ref[rows, :] * shrink + r[:, :D]

    def stretch_range(i):
        index = lax.broadcasted_iota(jnp.int32, (RB, 1), 0) + i * RB
        own = i < 4
        near = i < 8
        home_zh = jnp.where(own, zh, jnp.where(near, zh + jnp.where(is_pre, 3, 1), zh + 2))
        home_zh = lax.rem(home_zh, 4)
        index = index - jnp.where(own, 0, jnp.where(near, 1024, jnp.where(is_pre, 2048 - half, 2048)))
        place = (home_zh * 4 + y) * 128 + index // 8
        begin = jnp.zeros_like(place)
        for e in ends[:-1]:
            begin = jnp.where(place >= e, e, begin)
        return begin, place

    first_row = seq * 32

    def fresh_block(i, _):
        rows = block(0, i)
        index = lax.broadcasted_iota(jnp.int32, (RB, D), 0) + i * RB
        key = lax.broadcasted_iota(jnp.int32, (RB, D), 1)
        mask = (key // 4 == index // 32) & (lax.rem(key, 4) <= lax.rem(index // 8, 4))
        small(qall[rows, :], new_ref[...], mask, rows, m, l, acc)
        return 0

    def cache_rows(g, _):
        for u in range(4):
            r = g * 4 + u
            rows = pl.ds(pl.multiple_of(r * 32, 32), 32)
            length = cache_len_ref[first_row + r]
            mask = lax.broadcasted_iota(jnp.int32, (32, half), 1) < length
            small(qall[rows, :], cacheb[r], mask, rows, m, l, acc)
        return 0

    def second_copies():
        for c in kv_copies[:2]:
            c.wait_send()
        for c in stretch_y + kv_copies[2:4]:
            c.start()

    def decode_first():
        owner = lax.broadcasted_iota(jnp.int32, (256, 1), 0) // 32
        target = lax.rem(lax.broadcasted_iota(jnp.int32, (256, 1), 0), 32)
        for p in range(8):
            target = jnp.where(owner == p, target + (slots_ref[p] - first_row) * 32, target)
        chosen = lax.broadcasted_iota(jnp.int32, (256, 1024), 1) == target
        chosen = jnp.where(chosen, 1.0, 0.0).astype(BF16)
        pqall[0] = dot(chosen, qall[pl.ds(0, 1024), :], NN).astype(BF16)
        for c in p_copies:
            c.start()
        lax.fori_loop(0, 1024 // RB, fresh_block, 0)
        for g in range(4):
            cache_copy(g).wait()
        lax.fori_loop(0, 4, cache_rows, 0)
        stretch_z.wait_recv()
        second_copies()
        for g in range(4, 8):
            cache_copy(g).wait()
        lax.fori_loop(4, 8, cache_rows, 0)

    def prompt_part():
        for c in p_copies:
            c.wait_recv()
        pacc[...] = jnp.zeros_like(pacc)
        psum[...] = jnp.zeros_like(psum)
        pm[...] = jnp.full_like(pm, NEG)
        owner = lax.broadcasted_iota(jnp.int32, (256, 1), 0) // 32
        low = jnp.zeros_like(owner)
        high = jnp.zeros_like(owner)
        for p in range(8):
            low = jnp.where(owner == p, starts[p], low)
            high = jnp.where(owner == p, ends[p], high)
        keys = lax.broadcasted_iota(jnp.int32, (256, half), 1) + zh * half
        mask = (keys >= low) & (keys < high)

        def one(d, _):
            rows = block(0, d)
            small(pqall[d], kvb[pl.ds(2048, half), :], mask, rows, pm, psum, pacc)
            total = psum[rows, :]
            pob[d] = (pacc[rows, :] / total).astype(BF16)
            stat = pm[rows, :] + jnp.log2(total)
            pls[d] = jnp.zeros((8, D), F32)
            pls[d, pl.ds(0, 1), :] = jnp.transpose(stat[:D])[:1]
            pls[d, pl.ds(1, 1), :] = jnp.transpose(stat[D:])[:1]
            return 0

        lax.fori_loop(0, 4, one, 0)
        for c in p_back:
            c.start()

    def decode_last():
        for c in p_back:
            c.wait_recv()
        pback[0] = pob[0]
        plback[0] = pls[0]
        for b in range(2):
            rows = pl.ds(b * D, D)
            mixed, stat = weigh(
                [column(plback[d, pl.ds(b, 1), :]) for d in range(4)],
                [pback[d, rows, :].astype(F32) for d in range(4)],
            )
            pm[rows, :] = stat
            pacc[rows, :] = mixed

        def merge(r, _):
            rows = pl.ds(pl.multiple_of(r * 32, 32), 32)
            other = jnp.full((32, D), NEG, F32)
            value = jnp.zeros((32, D), F32)
            for p in range(8):
                theirs = pl.ds(p * 32, 32)
                hit = jnp.full((32, D), slots_ref[p] - first_row - r, jnp.int32) == 0
                other = jnp.where(hit, pm[theirs, :], other)
                value = jnp.where(hit, pacc[theirs, :], value)
            old = m[rows, :]
            new = jnp.maximum(old, other)
            w0 = jnp.exp2(old - new)
            w1 = jnp.exp2(other - new)
            mixed = acc[rows, :] * w0 + value * w1
            out_ref[rows, :] = (mixed / (l[rows, :] * w0 + w1)).astype(BF16)
            return 0

        lax.fori_loop(0, 32, merge, 0)

    far_o = ob.at[pl.ds(1024, half)]
    far_pre = [
        remote(far_o, rof, o_send.at[0], o_recv.at[0], 0, -2),
        remote(ls.at[2], rlf, l_send.at[0], l_recv.at[0], 0, -2),
    ]
    far_dec = [
        remote(far_o, rof, o_send.at[0], o_recv.at[0], 0, 2),
        remote(ls.at[2], rlf, l_send.at[0], l_recv.at[0], 0, 2),
    ]
    near_pre, near_dec = [], []
    for h in range(2):
        rows = pl.ds(h * half, half)
        near_pre.append([
            remote(ob.at[rows], ro.at[1, rows], o_send.at[1 + h], o_recv.at[3 + h], 0, -2),
            remote(ls.at[h], rl.at[1, h], l_send.at[1 + h], l_recv.at[3 + h], 0, -2),
        ])
        near_dec.append([
            remote(ob.at[rows], ro.at[0, rows], o_send.at[1 + h], o_recv.at[1 + h], 0, 1),
            remote(ls.at[h], rl.at[0, h], l_send.at[1 + h], l_recv.at[1 + h], 0, 1),
        ])

    def start_all(pre, dec):
        @pl.when(is_pre)
        def _():
            for c in pre:
                c.start()

        @pl.when(is_dec)
        def _():
            for c in dec:
                c.start()

    def finish_block(b, _):
        rows = pl.ds(pl.multiple_of(1024 + b * D, D), D)
        total = l[rows, :]
        ob[pl.ds(pl.multiple_of(b * D, D), D), :] = (acc[rows, :] / total).astype(BF16)
        stat = jnp.transpose(m[rows, :] + jnp.log2(total))
        ls[b // 4, pl.ds(lax.rem(b, 4), 1), :] = stat[:1, :]
        return 0

    def merge_block(b, _):
        rows = pl.ds(pl.multiple_of(1024 + b * D, D), D)
        theirs = lax.rem(b, 4)
        total = l[rows, :]
        mixed, stat = weigh(
            [m[rows, :] + jnp.log2(total), column(rlf[pl.ds(theirs, 1), :])],
            [acc[rows, :] / total, rof[pl.ds(pl.multiple_of(theirs * D, D), D), :].astype(F32)],
        )
        ob[pl.ds(pl.multiple_of(b * D, D), D), :] = mixed.astype(BF16)
        ls[b // 4, pl.ds(theirs, 1), :] = jnp.transpose(stat)[:1, :]
        return 0

    def send_far():
        ls[...] = jnp.zeros_like(ls)
        lax.fori_loop(8, 12, finish_block, 0)
        start_all(far_pre, far_dec)

    def send_near():
        first_block = jnp.where(is_pre, 0, 4)
        lax.fori_loop(first_block, first_block + 4, finish_block, 0)
        start_all(near_pre[0], near_dec[1])

    def send_merged():
        for c in far_pre:
            c.wait_recv()
        first_block = jnp.where(is_pre, 4, 0)
        lax.fori_loop(first_block, first_block + 4, merge_block, 0)
        start_all(near_pre[1], near_dec[0])

    def combine():
        for c in near_dec[1] + near_pre[0] + near_dec[0] + near_pre[1]:
            c.wait_recv()

        def one(b, _):
            rows = pl.ds(pl.multiple_of(b * D, D), D)
            total = l[rows, :]
            stats = [m[rows, :] + jnp.log2(total)]
            values = [acc[rows, :] / total]
            for i in range(2):
                stats.append(column(rl[i, b // 4, pl.ds(lax.rem(b, 4), 1), :]))
                values.append(ro[i, rows, :].astype(F32))
            mixed, _ = weigh(stats, values)
            out_ref[rows, :] = mixed.astype(BF16)
            return 0

        lax.fori_loop(0, 8, one, 0)

    @pl.when(is_pre)
    def _():
        attend(0, 4, 0, 1024)
        second_copies()

    @pl.when(is_dec)
    def _():
        decode_first()

    for c in kv_copies[:2]:
        c.wait_recv()
    q_copies[0].wait_recv()
    start_all([far_q_pre], [far_q_dec])

    def wide(i, _):
        @pl.when(i == 1)
        def _():
            for c in kv_copies[4:]:
                c.start()
            far_q_pre.wait_recv()

        attend(4 + 4 * i, 4 - 2 * i, 0, 2048)
        return 0

    lax.fori_loop(0, 2, wide, 0)
    for c in stretch_y + kv_copies[2:4]:
        c.wait_recv()
    attend(4, 6, 2048, 1536, 0)
    for c in kv_copies[4:]:
        c.wait_recv()

    def narrow(i, _):
        attend(8 - 4 * i, 2 + 2 * i, 3584, 1024)

        @pl.when(i == 0)
        def _():
            send_far()

        return 0

    lax.fori_loop(0, 2, narrow, 0)
    send_near()

    @pl.when(is_dec)
    def _():
        prompt_part()

    def rest(i, _):
        @pl.when(is_pre)
        def _():
            attend(2 * i, 2, 1024, 3584, 1024)

        @pl.when(i == 0)
        def _():
            send_merged()

        return 0

    lax.fori_loop(0, 2, rest, 0)

    @pl.when(is_pre)
    def _():
        combine()

    @pl.when(is_dec)
    def _():
        decode_last()

    for c in kv_copies[2:] + stretch_y + [far_q_pre] + far_pre + near_pre[0] + near_pre[1]:
        c.wait_send()

    @pl.when(is_pre)
    def _():
        for c in [stretch_z] + q_copies:
            c.wait_send()

    @pl.when(is_dec)
    def _():
        for c in p_copies + p_back:
            c.wait_send()


def body(queries, new_kv, prefix_kv, cache_kv, prompt_lengths, cache_lengths, prompt_slots):
    q = queries.reshape(1024, D)
    new = new_kv.reshape(128, 2 * D)
    prefix = prefix_kv.reshape(1024, 2 * D)
    cache = cache_kv.reshape(32, 512, 2 * D)
    vmem = pl.BlockSpec(memory_space=pltpu.VMEM)
    hbm = pl.BlockSpec(memory_space=pl.ANY)
    dma = pltpu.SemaphoreType.DMA
    out = pl.pallas_call(
        kernel,
        out_shape=jax.ShapeDtypeStruct((1024, D), BF16),
        in_specs=[hbm] * 7,
        out_specs=vmem,
        scratch_shapes=[
            pltpu.VMEM((4608, 2 * D), BF16),
            pltpu.VMEM((2560, D), BF16),
            pltpu.VMEM((2560, D), F32),
            pltpu.VMEM((2560, D), F32),
            pltpu.VMEM((2560, D), F32),
            pltpu.VMEM((1536, D), BF16),
            pltpu.VMEM((3, 8, D), F32),
            pltpu.VMEM((2, 1024, D), BF16),
            pltpu.VMEM((2, 2, 8, D), F32),
            pltpu.VMEM((512, D), BF16),
            pltpu.VMEM((8, D), F32),
            pltpu.VMEM((32, 512, 2 * D), BF16),
            pltpu.VMEM((RB, 3584), F32),
            pltpu.VMEM((RB, 3584), F32),
            pltpu.VMEM((RB, D), F32),
            pltpu.VMEM((RB, D), F32),
            pltpu.VMEM((4, 256, D), BF16),
            pltpu.VMEM((1024, D), F32),
            pltpu.VMEM((1024, D), F32),
            pltpu.VMEM((1024, D), F32),
            pltpu.VMEM((4, 256, D), BF16),
            pltpu.VMEM((4, 8, D), F32),
            pltpu.VMEM((4, 256, D), BF16),
            pltpu.VMEM((4, 8, D), F32),
            pltpu.VMEM((128, 2 * D), BF16),
            pltpu.SMEM((8,), jnp.int32),
            pltpu.SMEM((512,), jnp.int32),
            pltpu.SMEM((8,), jnp.int32),
            dma((6,)), dma((8,)), dma((6,)), dma((6,)), dma((3,)), dma((2,)),
            dma((4,)), dma((4,)), dma((3,)), dma((3,)), dma((3, 2)), dma((3, 2)),
            dma((3,)), dma((5,)), dma((3,)), dma((5,)),
        ],
        compiler_params=pltpu.CompilerParams(
            collective_id=0, has_side_effects=True, vmem_limit_bytes=62 * 2**20
        ),
        cost_estimate=pl.CostEstimate(flops=10**10, bytes_accessed=10**7, transcendentals=10**7),
    )(prompt_lengths, cache_lengths, prompt_slots, q, new, prefix, cache)
    return out.reshape(1, 128, 1024)


def solution(mesh):
    return jax.shard_map(
        body,
        mesh=mesh,
        in_specs=(
            P("role", "seq", "tensor"),
            P("role", "seq", "tensor", None),
            P("seq", "tensor", None),
            P("seq", None, "tensor", None),
            P(),
            P(),
            P(),
        ),
        out_specs=P("role", "seq", "tensor"),
        check_vma=False,
    )
```

```python
import functools
import math

import jax
import jax.numpy as jnp
from jax import lax
from jax.experimental import pallas as pl
from jax.experimental.pallas import tpu as pltpu
from jax.sharding import PartitionSpec as P

MESH = pl.DeviceIdType.MESH
NEG = -1e30
D = 128
SCALE = math.log2(math.e) / math.sqrt(D)
RB = 256
NT = (((1,), (1,)), ((), ()))
NN = (((1,), (0,)), ((), ()))
F32 = jnp.float32
BF16 = jnp.bfloat16


def dot(a, b, dims):
    return lax.dot_general(a, b, dims, preferred_element_type=F32)


def with_ones(v):
    return jnp.concatenate([v, jnp.ones_like(v)], axis=1)


def column(row):
    return jnp.transpose(jnp.broadcast_to(row, (D, D)))


def kernel(
    lengths_hbm, cache_len_hbm, slots_hbm, q_ref, new_hbm, prefix_ref, cache_ref,
    out_ref,
    kvb, qall, acc, m, l, ob, ls, ro, rl, rof, rlf, cacheb, sa, sb, ma, mb,
    pqall, pacc, pm, psum, pob, pls, pback, plback, new_ref, lengths_ref, cache_len_ref, slots_ref,
    local_sem, cache_sem, kv_send, kv_recv, q_send, q_recv, str_send, str_recv,
    p_send, p_recv, pb_send, pb_recv, o_send, o_recv, l_send, l_recv,
):
    role = lax.axis_index("role")
    seq = lax.axis_index("seq")
    tensor = lax.axis_index("tensor")
    zh, y = seq // 4, lax.rem(seq, 4)
    z = zh * 2 + role

    def dev(dy, dz):
        yy = lax.rem(y + dy + 8, 4)
        zz = lax.rem(z + dz + 8, 8)
        return (lax.rem(zz, 2), (zz // 2) * 4 + yy, tensor)

    def remote(src, dst, ss, rs, dy, dz):
        return pltpu.make_async_remote_copy(
            src_ref=src, dst_ref=dst, send_sem=ss, recv_sem=rs,
            device_id=dev(dy, dz), device_id_type=MESH,
        )

    is_pre = role == 0
    is_dec = role == 1
    half = 512

    own_kv = pltpu.make_async_copy(prefix_ref, kvb.at[pl.ds(0, 1024)], local_sem.at[0])
    own_kv.start()
    own_q = pltpu.make_async_copy(q_ref, qall.at[pl.ds(0, 1024)], local_sem.at[1])
    own_q.start()
    own_new = pltpu.make_async_copy(new_hbm, new_ref, local_sem.at[2])
    own_new.start()
    scalars = [
        pltpu.make_async_copy(lengths_hbm, lengths_ref, local_sem.at[3]),
        pltpu.make_async_copy(cache_len_hbm, cache_len_ref, local_sem.at[4]),
        pltpu.make_async_copy(slots_hbm, slots_ref, local_sem.at[5]),
    ]
    for c in scalars:
        c.start()

    def cache_copy(g):
        rows = pl.ds(g * 4, 4)
        return pltpu.make_async_copy(cache_ref.at[rows], cacheb.at[rows], cache_sem.at[g])

    barrier = pltpu.get_barrier_semaphore()
    peers = [(0, dz) for dz in (1, 2, 4, 6, 7)] + [(1, 0), (2, 0), (3, 0)]
    for dy, dz in peers:
        pl.semaphore_signal(barrier, inc=1, device_id=dev(dy, dz), device_id_type=MESH)
    def clear(b, _):
        rows = pl.ds(pl.multiple_of(b * D, D), D)
        acc[rows, :] = jnp.zeros((D, D), F32)
        l[rows, :] = jnp.zeros((D, D), F32)
        m[rows, :] = jnp.full((D, D), NEG, F32)
        return 0

    lax.fori_loop(0, 20, clear, 0)

    own_kv.wait()
    own_new.wait()
    own_q.wait()
    for c in scalars:
        c.wait()
    pl.semaphore_wait(barrier, len(peers))

    own_stretch = pl.ds(pl.multiple_of(2 * 1024 + y * 128, 128), 128)
    slot = kvb.at[own_stretch]
    stretch_y = [remote(slot, slot, str_send.at[i], str_recv.at[i], dy, 0) for i, dy in enumerate((1, 3, 2))]
    stretch_z = remote(slot, slot, str_send.at[3], str_recv.at[3], 0, 1)
    def part(piece, h):
        return kvb.at[pl.ds((0, 1024, 2560, 3584)[piece] + h * half, half)]

    kv_copies = [
        remote(part(0, 0), part(1, 0), kv_send.at[0], kv_recv.at[0], 1, 0),
        remote(part(0, 1), part(1, 1), kv_send.at[1], kv_recv.at[1], 3, 0),
        remote(part(0, 1), part(2, 0), kv_send.at[2], kv_recv.at[2], 1, 0),
        remote(part(0, 0), part(2, 1), kv_send.at[3], kv_recv.at[3], 3, 0),
        remote(part(1, 0), part(3, 0), kv_send.at[4], kv_recv.at[4], 1, 0),
        remote(part(1, 1), part(3, 1), kv_send.at[5], kv_recv.at[5], 3, 0),
    ]
    home_q, near_q = qall.at[pl.ds(0, 1024)], qall.at[pl.ds(1024, 1024)]
    far_q = qall.at[pl.ds(2048, half)]
    q_copies = [
        remote(home_q, near_q, q_send.at[0], q_recv.at[0], 0, -1),
        remote(home_q, near_q, q_send.at[1], q_recv.at[0], 0, 2),
    ]
    far_q_pre = remote(qall.at[pl.ds(1024 + half, half)], far_q, q_send.at[2], q_recv.at[1], 0, 2)
    far_q_dec = remote(qall.at[pl.ds(1024, half)], far_q, q_send.at[2], q_recv.at[1], 0, -2)
    p_copies = [
        remote(pqall.at[0], pqall.at[d], p_send.at[d - 1], p_recv.at[d - 1], 0, 2 * d) for d in (1, 2, 3)
    ]
    p_back = []
    for d in (1, 2, 3):
        p_back.append(remote(pob.at[d], pback.at[d], pb_send.at[d - 1, 0], pb_recv.at[d - 1, 0], 0, -2 * d))
        p_back.append(remote(pls.at[d], plback.at[d], pb_send.at[d - 1, 1], pb_recv.at[d - 1, 1], 0, -2 * d))

    @pl.when(is_pre)
    def _():
        kvb[own_stretch, :] = new_ref[...]
        stretch_z.start()

    for c in kv_copies[:2]:
        c.start()

    @pl.when(is_pre)
    def _():
        for c in q_copies:
            c.start()

    @pl.when(is_dec)
    def _():
        for g in range(8):
            cache_copy(g).start()

    def block(row0, i):
        return pl.ds(pl.multiple_of(row0 + i * RB, RB), RB)

    def scores(b, k0, span, masked, s, mx):
        rows = block(0, b)
        x = dot(qall[rows, :], kvb[pl.ds(k0, span), :D], NT)
        s[:, :span] = x
        if masked is None:
            top = jnp.max(x, axis=1, keepdims=True)
        else:
            begin, place = stretch_range(b)
            keys = lax.broadcasted_iota(jnp.int32, (RB, half), 1) + zh * half
            y0 = jnp.where((keys >= begin) & (keys <= place), x[:, masked : masked + half], NEG)
            s[:, masked : masked + half] = y0
            top = jnp.max(y0, axis=1, keepdims=True)
            if masked:
                top = jnp.maximum(top, jnp.max(x[:, :masked], axis=1, keepdims=True))
            if masked + half < span:
                top = jnp.maximum(top, jnp.max(x[:, masked + half :], axis=1, keepdims=True))
        mx[...] = jnp.broadcast_to(top * SCALE, mx.shape)

    def absorb(b, k0, span, s, mx):
        rows = block(0, b)
        old = m[rows, :]
        new = jnp.maximum(old, mx[...])
        shrink = jnp.exp2(old - new)
        m[rows, :] = new
        p = jnp.exp2(s[:, :span] * SCALE - new[:, :1]).astype(BF16)
        r = dot(p, with_ones(kvb[pl.ds(k0, span), D:]), NN)
        l[rows, :] = l[rows, :] * shrink + r[:, D:]
        acc[rows, :] = acc[rows, :] * shrink + r[:, :D]

    def attend(b0, n, k0, span, masked=None):
        scores(b0, k0, span, masked, sa, ma)

        def pair(j, _):
            b = b0 + 2 * j
            scores(b + 1, k0, span, masked, sb, mb)
            absorb(b, k0, span, sa, ma)
            scores(jnp.minimum(b + 2, b0 + n - 1), k0, span, masked, sa, ma)
            absorb(b + 1, k0, span, sb, mb)
            return 0

        lax.fori_loop(0, n // 2, pair, 0)

    def weigh(stats, values):
        top = functools.reduce(jnp.maximum, stats)
        weights = [jnp.exp2(x - top) for x in stats]
        total = functools.reduce(jnp.add, weights)
        mixed = functools.reduce(jnp.add, [w * v for w, v in zip(weights, values)])
        return mixed / total, top + jnp.log2(total)

    ends = []
    running = jnp.int32(0)
    for p in range(8):
        running = running + lengths_ref[p]
        ends.append(running)
    starts = [jnp.int32(0)] + ends[:-1]

    def small(qv, kv_value, mask, rows, m_ref, l_ref, acc_ref):
        s = jnp.where(mask, dot(qv, kv_value[:, :D], NT) * SCALE, NEG)
        old = m_ref[rows, :]
        new = jnp.maximum(old, jnp.max(s, axis=1, keepdims=True))
        shrink = jnp.exp2(old - new)
        p = jnp.exp2(s - new[:, :1]).astype(BF16)
        r = dot(p, with_ones(kv_value[:, D:]), NN)
        m_ref[rows, :] = new
        l_ref[rows, :] = l_ref[rows, :] * shrink + r[:, D:]
        acc_ref[rows, :] = acc_ref[rows, :] * shrink + r[:, :D]

    def stretch_range(i):
        index = lax.broadcasted_iota(jnp.int32, (RB, 1), 0) + i * RB
        own = i < 4
        near = i < 8
        home_zh = jnp.where(own, zh, jnp.where(near, zh + jnp.where(is_pre, 3, 1), zh + 2))
        home_zh = lax.rem(home_zh, 4)
        index = index - jnp.where(own, 0, jnp.where(near, 1024, jnp.where(is_pre, 2048 - half, 2048)))
        place = (home_zh * 4 + y) * 128 + index // 8
        begin = jnp.zeros_like(place)
        for e in ends[:-1]:
            begin = jnp.where(place >= e, e, begin)
        return begin, place

    first_row = seq * 32

    def fresh_block(i, _):
        rows = block(0, i)
        index = lax.broadcasted_iota(jnp.int32, (RB, D), 0) + i * RB
        key = lax.broadcasted_iota(jnp.int32, (RB, D), 1)
        mask = (key // 4 == index // 32) & (lax.rem(key, 4) <= lax.rem(index // 8, 4))
        small(qall[rows, :], new_ref[...], mask, rows, m, l, acc)
        return 0

    def cache_rows(g, _):
        for u in range(4):
            r = g * 4 + u
            rows = pl.ds(pl.multiple_of(r * 32, 32), 32)
            length = cache_len_ref[first_row + r]
            mask = lax.broadcasted_iota(jnp.int32, (32, half), 1) < length
            small(qall[rows, :], cacheb[r], mask, rows, m, l, acc)
        return 0

    def second_copies():
        for c in kv_copies[:2]:
            c.wait_send()
        for c in stretch_y + kv_copies[2:4]:
            c.start()

    def decode_first():
        owner = lax.broadcasted_iota(jnp.int32, (256, 1), 0) // 32
        target = lax.rem(lax.broadcasted_iota(jnp.int32, (256, 1), 0), 32)
        for p in range(8):
            target = jnp.where(owner == p, target + (slots_ref[p] - first_row) * 32, target)
        chosen = lax.broadcasted_iota(jnp.int32, (256, 1024), 1) == target
        chosen = jnp.where(chosen, 1.0, 0.0).astype(BF16)
        pqall[0] = dot(chosen, qall[pl.ds(0, 1024), :], NN).astype(BF16)
        for c in p_copies:
            c.start()
        lax.fori_loop(0, 1024 // RB, fresh_block, 0)
        for g in range(4):
            cache_copy(g).wait()
        lax.fori_loop(0, 4, cache_rows, 0)
        stretch_z.wait_recv()
        second_copies()
        for g in range(4, 8):
            cache_copy(g).wait()
        lax.fori_loop(4, 8, cache_rows, 0)

    def prompt_part():
        for c in p_copies:
            c.wait_recv()
        pacc[...] = jnp.zeros_like(pacc)
        psum[...] = jnp.zeros_like(psum)
        pm[...] = jnp.full_like(pm, NEG)
        owner = lax.broadcasted_iota(jnp.int32, (256, 1), 0) // 32
        low = jnp.zeros_like(owner)
        high = jnp.zeros_like(owner)
        for p in range(8):
            low = jnp.where(owner == p, starts[p], low)
            high = jnp.where(owner == p, ends[p], high)
        keys = lax.broadcasted_iota(jnp.int32, (256, half), 1) + zh * half
        mask = (keys >= low) & (keys < high)

        def one(d, _):
            rows = block(0, d)
            small(pqall[d], kvb[pl.ds(2048, half), :], mask, rows, pm, psum, pacc)
            total = psum[rows, :]
            pob[d] = (pacc[rows, :] / total).astype(BF16)
            stat = pm[rows, :] + jnp.log2(total)
            pls[d] = jnp.zeros((8, D), F32)
            pls[d, pl.ds(0, 1), :] = jnp.transpose(stat[:D])[:1]
            pls[d, pl.ds(1, 1), :] = jnp.transpose(stat[D:])[:1]
            return 0

        lax.fori_loop(0, 4, one, 0)
        for c in p_back:
            c.start()

    def decode_last():
        for c in p_back:
            c.wait_recv()
        pback[0] = pob[0]
        plback[0] = pls[0]
        for b in range(2):
            rows = pl.ds(b * D, D)
            mixed, stat = weigh(
                [column(plback[d, pl.ds(b, 1), :]) for d in range(4)],
                [pback[d, rows, :].astype(F32) for d in range(4)],
            )
            pm[rows, :] = stat
            pacc[rows, :] = mixed

        def merge(r, _):
            rows = pl.ds(pl.multiple_of(r * 32, 32), 32)
            other = jnp.full((32, D), NEG, F32)
            value = jnp.zeros((32, D), F32)
            for p in range(8):
                theirs = pl.ds(p * 32, 32)
                hit = jnp.full((32, D), slots_ref[p] - first_row - r, jnp.int32) == 0
                other = jnp.where(hit, pm[theirs, :], other)
                value = jnp.where(hit, pacc[theirs, :], value)
            old = m[rows, :]
            new = jnp.maximum(old, other)
            w0 = jnp.exp2(old - new)
            w1 = jnp.exp2(other - new)
            mixed = acc[rows, :] * w0 + value * w1
            out_ref[rows, :] = (mixed / (l[rows, :] * w0 + w1)).astype(BF16)
            return 0

        lax.fori_loop(0, 32, merge, 0)

    far_o = ob.at[pl.ds(1024, half)]
    far_pre = [
        remote(far_o, rof, o_send.at[0], o_recv.at[0], 0, -2),
        remote(ls.at[2], rlf, l_send.at[0], l_recv.at[0], 0, -2),
    ]
    far_dec = [
        remote(far_o, rof, o_send.at[0], o_recv.at[0], 0, 2),
        remote(ls.at[2], rlf, l_send.at[0], l_recv.at[0], 0, 2),
    ]
    near_pre, near_dec = [], []
    for h in range(2):
        rows = pl.ds(h * half, half)
        near_pre.append([
            remote(ob.at[rows], ro.at[1, rows], o_send.at[1 + h], o_recv.at[3 + h], 0, -2),
            remote(ls.at[h], rl.at[1, h], l_send.at[1 + h], l_recv.at[3 + h], 0, -2),
        ])
        near_dec.append([
            remote(ob.at[rows], ro.at[0, rows], o_send.at[1 + h], o_recv.at[1 + h], 0, 1),
            remote(ls.at[h], rl.at[0, h], l_send.at[1 + h], l_recv.at[1 + h], 0, 1),
        ])

    def start_all(pre, dec):
        @pl.when(is_pre)
        def _():
            for c in pre:
                c.start()

        @pl.when(is_dec)
        def _():
            for c in dec:
                c.start()

    def finish_block(b, _):
        rows = pl.ds(pl.multiple_of(1024 + b * D, D), D)
        total = l[rows, :]
        ob[pl.ds(pl.multiple_of(b * D, D), D), :] = (acc[rows, :] / total).astype(BF16)
        stat = jnp.transpose(m[rows, :] + jnp.log2(total))
        ls[b // 4, pl.ds(lax.rem(b, 4), 1), :] = stat[:1, :]
        return 0

    def merge_block(b, _):
        rows = pl.ds(pl.multiple_of(1024 + b * D, D), D)
        theirs = lax.rem(b, 4)
        total = l[rows, :]
        mixed, stat = weigh(
            [m[rows, :] + jnp.log2(total), column(rlf[pl.ds(theirs, 1), :])],
            [acc[rows, :] / total, rof[pl.ds(pl.multiple_of(theirs * D, D), D), :].astype(F32)],
        )
        ob[pl.ds(pl.multiple_of(b * D, D), D), :] = mixed.astype(BF16)
        ls[b // 4, pl.ds(theirs, 1), :] = jnp.transpose(stat)[:1, :]
        return 0

    def send_far():
        ls[...] = jnp.zeros_like(ls)
        lax.fori_loop(8, 12, finish_block, 0)
        start_all(far_pre, far_dec)

    def send_near():
        first_block = jnp.where(is_pre, 0, 4)
        lax.fori_loop(first_block, first_block + 4, finish_block, 0)
        start_all(near_pre[0], near_dec[1])

    def send_merged():
        for c in far_pre:
            c.wait_recv()
        first_block = jnp.where(is_pre, 4, 0)
        lax.fori_loop(first_block, first_block + 4, merge_block, 0)
        start_all(near_pre[1], near_dec[0])

    def combine():
        for c in near_dec[1] + near_pre[0] + near_dec[0] + near_pre[1]:
            c.wait_recv()

        def one(b, _):
            rows = pl.ds(pl.multiple_of(b * D, D), D)
            total = l[rows, :]
            stats = [m[rows, :] + jnp.log2(total)]
            values = [acc[rows, :] / total]
            for i in range(2):
                stats.append(column(rl[i, b // 4, pl.ds(lax.rem(b, 4), 1), :]))
                values.append(ro[i, rows, :].astype(F32))
            mixed, _ = weigh(stats, values)
            out_ref[rows, :] = mixed.astype(BF16)
            return 0

        lax.fori_loop(0, 8, one, 0)

    @pl.when(is_pre)
    def _():
        attend(0, 4, 0, 1024)
        second_copies()

    @pl.when(is_dec)
    def _():
        decode_first()

    for c in kv_copies[:2]:
        c.wait_recv()
    for c in kv_copies[4:]:
        c.start()
    q_copies[0].wait_recv()
    start_all([far_q_pre], [far_q_dec])

    def wide(i, _):
        @pl.when(i == 1)
        def _():
            far_q_pre.wait_recv()

        attend(4 + 4 * i, 4 - 2 * i, 0, 2048)
        return 0

    lax.fori_loop(0, 2, wide, 0)
    for c in stretch_y + kv_copies[2:4]:
        c.wait_recv()
    attend(4, 6, 2048, 1536, 0)
    for c in kv_copies[4:]:
        c.wait_recv()

    def narrow(i, _):
        attend(8 - 4 * i, 2 + 2 * i, 3584, 1024)

        @pl.when(i == 0)
        def _():
            send_far()

        return 0

    lax.fori_loop(0, 2, narrow, 0)
    send_near()

    @pl.when(is_dec)
    def _():
        prompt_part()

    def rest(i, _):
        @pl.when(is_pre)
        def _():
            attend(2 * i, 2, 1024, 3584, 1024)

        @pl.when(i == 0)
        def _():
            send_merged()

        return 0

    lax.fori_loop(0, 2, rest, 0)

    @pl.when(is_pre)
    def _():
        combine()

    @pl.when(is_dec)
    def _():
        decode_last()

    for c in kv_copies[2:] + stretch_y + [far_q_pre] + far_pre + near_pre[0] + near_pre[1]:
        c.wait_send()

    @pl.when(is_pre)
    def _():
        for c in [stretch_z] + q_copies:
            c.wait_send()

    @pl.when(is_dec)
    def _():
        for c in p_copies + p_back:
            c.wait_send()


def body(queries, new_kv, prefix_kv, cache_kv, prompt_lengths, cache_lengths, prompt_slots):
    q = queries.reshape(1024, D)
    new = new_kv.reshape(128, 2 * D)
    prefix = prefix_kv.reshape(1024, 2 * D)
    cache = cache_kv.reshape(32, 512, 2 * D)
    vmem = pl.BlockSpec(memory_space=pltpu.VMEM)
    hbm = pl.BlockSpec(memory_space=pl.ANY)
    dma = pltpu.SemaphoreType.DMA
    out = pl.pallas_call(
        kernel,
        out_shape=jax.ShapeDtypeStruct((1024, D), BF16),
        in_specs=[hbm] * 7,
        out_specs=vmem,
        scratch_shapes=[
            pltpu.VMEM((4608, 2 * D), BF16),
            pltpu.VMEM((2560, D), BF16),
            pltpu.VMEM((2560, D), F32),
            pltpu.VMEM((2560, D), F32),
            pltpu.VMEM((2560, D), F32),
            pltpu.VMEM((1536, D), BF16),
            pltpu.VMEM((3, 8, D), F32),
            pltpu.VMEM((2, 1024, D), BF16),
            pltpu.VMEM((2, 2, 8, D), F32),
            pltpu.VMEM((512, D), BF16),
            pltpu.VMEM((8, D), F32),
            pltpu.VMEM((32, 512, 2 * D), BF16),
            pltpu.VMEM((RB, 3584), F32),
            pltpu.VMEM((RB, 3584), F32),
            pltpu.VMEM((RB, D), F32),
            pltpu.VMEM((RB, D), F32),
            pltpu.VMEM((4, 256, D), BF16),
            pltpu.VMEM((1024, D), F32),
            pltpu.VMEM((1024, D), F32),
            pltpu.VMEM((1024, D), F32),
            pltpu.VMEM((4, 256, D), BF16),
            pltpu.VMEM((4, 8, D), F32),
            pltpu.VMEM((4, 256, D), BF16),
            pltpu.VMEM((4, 8, D), F32),
            pltpu.VMEM((128, 2 * D), BF16),
            pltpu.SMEM((8,), jnp.int32),
            pltpu.SMEM((512,), jnp.int32),
            pltpu.SMEM((8,), jnp.int32),
            dma((6,)), dma((8,)), dma((6,)), dma((6,)), dma((3,)), dma((2,)),
            dma((4,)), dma((4,)), dma((3,)), dma((3,)), dma((3, 2)), dma((3, 2)),
            dma((3,)), dma((5,)), dma((3,)), dma((5,)),
        ],
        compiler_params=pltpu.CompilerParams(
            collective_id=0, has_side_effects=True, vmem_limit_bytes=62 * 2**20
        ),
        cost_estimate=pl.CostEstimate(flops=10**10, bytes_accessed=10**7, transcendentals=10**7),
    )(prompt_lengths, cache_lengths, prompt_slots, q, new, prefix, cache)
    return out.reshape(1, 128, 1024)


def solution(mesh):
    return jax.shard_map(
        body,
        mesh=mesh,
        in_specs=(
            P("role", "seq", "tensor"),
            P("role", "seq", "tensor", None),
            P("seq", "tensor", None),
            P("seq", None, "tensor", None),
            P(),
            P(),
            P(),
        ),
        out_specs=P("role", "seq", "tensor"),
        check_vma=False,
    )
```
